32 devices in a mesh: gx: 4 (over y, core), gy: 8 (over z, x).
Axes of the slice: x: 2, y: 2, z: 4, core: 2. Of those that a mesh axis runs over, the one named last changes fastest.
Arguments:
- inputs: bfloat16 [1536, 7168], P('gy', 'gx'), may hold values from -6 to 6
- query_weight: bfloat16 [1792, 7168], P('gy', 'gx'), may hold values from -0.0625 to 0.0625
- key_weight: bfloat16 [1792, 7168], P('gy', 'gx'), may hold values from -0.0625 to 0.0625
- value_weight: bfloat16 [1792, 7168], P('gy', 'gx'), may hold values from -0.0625 to 0.0625
- adapter_down: bfloat16 [128, 7168], P(None, 'gx'), may hold values from -0.0625 to 0.0625
- adapter_up: bfloat16 [1792, 128], P('gy'), may hold values from -0.5 to 0.5
- prompt_keys: bfloat16 [4, 1792, 2048], P('gx', 'gy'), may hold values from -6 to 6
- prompt_values: bfloat16 [4, 1792, 2048], P('gx', 'gy'), may hold values from -6 to 6
- cache_keys: bfloat16 [32, 1792, 512], P('gx', 'gy'), may hold values from -240 to 240
- cache_values: bfloat16 [32, 1792, 512], P('gx', 'gy'), may hold values from -6 to 6
- cache_lengths: int32 [32], P('gx'), may hold values from 1 to 512, as said below
- parents: int32 [32, 48], P('gx'), may hold values from 0 to 46, as said below
- out_weight: bfloat16 [1792, 3584], P('gy', 'gx'), may hold values from -0.1875 to 0.1875
Outputs:
- layer_output: bfloat16 [1536, 3584], P('gx', 'gy')
The draws below stay inside these ranges and needn't reach their ends.
Inputs may be any that keep to these rules, and one draw needn't show every extreme that they name: `parents`: node n's parent is a node below n, node 0 is its own parent, and node 47 hangs from node 46. `cache_lengths`: some request has all 512 positions valid.
All inputs are finite; a program needn't handle non-finite values.
Results may differ from the reference program's by a relative error of at most 0.017.
Values may be sent and summed in bfloat16 or wider, within the bound.
A program may use at most 128 MiB of HBM per device.

```python
import math
import jax
import jax.numpy as jnp
from jax import lax

DIN = 7168
DM = 3584
HEAD = 224
RANK = 128
NODES = 48
REQ_DEV = 8
PROMPT = 2048
CACHE = 512
HEADS = 8
HD = 1792
GROUPS = 4
REQ = 32
TOKENS = 1536


def draw_parents(key, part):
    columns = jnp.arange(NODES, dtype=jnp.int32)
    ceiling = jnp.maximum(columns, 1)
    drawn = jax.random.randint(key, (REQ, NODES), 0, 1 << 20, dtype=jnp.int32)
    chosen = drawn % ceiling[None, :]
    return jnp.where(columns[None, :] == NODES - 1, NODES - 2, chosen).astype(jnp.int32)


def draw_cache_lengths(key, part):
    drawn = jax.random.randint(key, (REQ,), 1, CACHE + 1, dtype=jnp.int32)
    fullest = jax.random.randint(jax.random.fold_in(key, 7), (), 0, REQ, dtype=jnp.int32)
    return jnp.where(jnp.arange(REQ, dtype=jnp.int32) == fullest, CACHE, drawn).astype(jnp.int32)


def draw_cache_keys(key, part):
    values = jnp.clip(jax.random.normal(key, (REQ, HD, CACHE), jnp.float32), -6.0, 6.0)
    return values.astype(jnp.bfloat16)


def raised(entries, stream_key, source, target, shards_of, factor):
    def block_of(axis_at):
        return (jnp.arange(entries.shape[axis_at]) // (entries.shape[axis_at] // shards_of)).reshape((-1,) + (1,) * (entries.ndim - 1 - axis_at))

    first = jax.random.permutation(stream_key, shards_of)[block_of(target)]
    far = (block_of(target) + shards_of // 2) % shards_of
    return jnp.where((block_of(source) == first) | (block_of(source) == far), factor * entries, entries)


def shard_levels(rng, extent, shards, least, high):
    factor_of = 1.0
    for position, shards_of in shards:
        heights = jax.random.uniform(jax.random.fold_in(jax.random.fold_in(rng, 6), position), (shards_of,), jnp.float32, least / len(shards), high / len(shards))
        factor_of = factor_of * jnp.repeat(jnp.exp(heights), extent[position] // shards_of).reshape((-1,) + (1,) * (len(extent) - 1 - position))
    return factor_of


def noise(own_key, shape, scale, reach, shards=(), held_as=jnp.bfloat16):
    values = jax.random.normal(own_key, shape, jnp.float32) * scale
    if len(shards) > 0:
        values = shard_levels(own_key, shape, shards, -0.22, 0.18) * values
    return jnp.clip(values, min=-reach, max=reach).astype(held_as)


def gaussian_with(stream_key, extent, scale, most, cuts, heavy, held_as=jnp.bfloat16):
    values = scale * jax.random.normal(stream_key, extent, jnp.float32)
    if cuts:
        values = values * shard_levels(stream_key, extent, cuts, -0.22, 0.18)
    return jnp.clip(raised(values, jax.random.fold_in(stream_key, 3), *heavy), -most, most).astype(held_as)


def setup_inputs(seed: int = 0) -> dict:
    streams_of = jax.random.split(jax.random.key(seed), 14)
    return {
        "inputs": noise(streams_of[0], (TOKENS, DIN), 1.0, 6.0, ((0, 8), (1, 4))),
        "query_weight": noise(streams_of[1], (HD, DIN), DIN ** -0.5, 0.0625, ((0, 8), (1, 4))),
        "key_weight": noise(streams_of[2], (HD, DIN), DIN ** -0.5, 0.0625, ((0, 8), (1, 4))),
        "value_weight": noise(streams_of[3], (HD, DIN), DIN ** -0.5, 0.0625, ((0, 8), (1, 4))),
        "adapter_down": noise(streams_of[4], (RANK, DIN), DIN ** -0.5, 0.0625, ((1, 4),)),
        "adapter_up": noise(streams_of[5], (HD, RANK), RANK ** -0.5, 0.5, ((0, 8),)),
        "prompt_keys": noise(streams_of[6], (GROUPS, HD, PROMPT), 1.0, 6.0, ((0, 4), (1, 8))),
        "prompt_values": noise(streams_of[7], (GROUPS, HD, PROMPT), 1.0, 6.0, ((0, 4), (1, 8))),
        "cache_keys": draw_cache_keys(jax.random.fold_in(streams_of[13], 71), 0),
        "cache_values": noise(streams_of[9], (REQ, HD, CACHE), 1.0, 6.0, ((0, 4), (1, 8))),
        "cache_lengths": draw_cache_lengths(jax.random.fold_in(streams_of[13], 71), 0),
        "parents": draw_parents(jax.random.fold_in(streams_of[13], 71), 0),
        "out_weight": gaussian_with(streams_of[12], (HD, DM), HD ** -0.5, 0.1875, ((0, 8), (1, 4)), (0, 1, 8, 2.0)),
    }


def ancestors(parents):
    node_count = parents.shape[1]
    columns = jnp.arange(node_count, dtype=jnp.int32)
    parent_hot = (parents[:, :, None] == columns[None, None, :]).astype(jnp.float32)
    reached = jnp.minimum(jnp.eye(node_count, dtype=jnp.float32)[None] + parent_hot, 1.0)
    rounds = max(1, math.ceil(math.log2(node_count)))
    for sweep in range(rounds):
        reached = jnp.minimum(reached + jnp.einsum('rnm,rmk->rnk', reached, reached, precision=lax.Precision.HIGHEST), 1.0)
    return reached

def attend(queries, new_keys, new_values, prompt_k, prompt_v, cache_k, cache_v, lengths, parents):
    factor = 1.0 / math.sqrt(queries.shape[-1])
    query_f = queries.astype(jnp.float32)
    s_prompt = jnp.einsum('rnhe,hep->rnhp', query_f, prompt_k.astype(jnp.float32)) * factor
    s_cache = jnp.einsum('rnhe,rhec->rnhc', query_f, cache_k.astype(jnp.float32)) * factor
    s_tree = jnp.einsum('rnhe,rmhe->rnhm', query_f, new_keys.astype(jnp.float32)) * factor
    usable = jnp.arange(cache_k.shape[-1], dtype=jnp.int32)[None, :] < lengths[:, None]
    s_cache = jnp.where(usable[:, None, None, :], s_cache, -jnp.inf)
    reached = ancestors(parents)
    s_tree = jnp.where(reached[:, :, None, :] > 0.5, s_tree, -jnp.inf)
    largest = jnp.maximum(jnp.maximum(lax.optimization_barrier(jnp.max(s_prompt, axis=-1, keepdims=True)), lax.optimization_barrier(jnp.max(s_cache, axis=-1, keepdims=True))), lax.optimization_barrier(jnp.max(s_tree, axis=-1, keepdims=True)))
    e_prompt = jnp.exp(s_prompt - largest)
    e_cache = jnp.exp(s_cache - largest)
    e_tree = jnp.exp(s_tree - largest)
    totals = lax.optimization_barrier(jnp.sum(e_prompt, axis=-1, keepdims=True)) + lax.optimization_barrier(jnp.sum(e_cache, axis=-1, keepdims=True)) + lax.optimization_barrier(jnp.sum(e_tree, axis=-1, keepdims=True))
    w_prompt = (e_prompt / totals).astype(jnp.bfloat16).astype(jnp.float32)
    w_cache = (e_cache / totals).astype(jnp.bfloat16).astype(jnp.float32)
    w_tree = (e_tree / totals).astype(jnp.bfloat16).astype(jnp.float32)
    result = jnp.einsum('rnhp,hep->rnhe', w_prompt, prompt_v.astype(jnp.float32))
    result = result + jnp.einsum('rnhc,rhec->rnhe', w_cache, cache_v.astype(jnp.float32))
    result = result + jnp.einsum('rnhm,rmhe->rnhe', w_tree, new_values.astype(jnp.float32))
    return result.astype(jnp.bfloat16)

def reference(inputs, query_weight, key_weight, value_weight, adapter_down, adapter_up, prompt_keys, prompt_values, cache_keys, cache_values, cache_lengths, parents, out_weight):
    query_base = jnp.dot(inputs, query_weight.T, preferred_element_type=jnp.float32)
    new_keys = jnp.dot(inputs, key_weight.T, preferred_element_type=jnp.float32).astype(jnp.bfloat16)
    new_values = jnp.dot(inputs, value_weight.T, preferred_element_type=jnp.float32).astype(jnp.bfloat16)
    adapter_mid = jnp.dot(inputs, adapter_down.T, preferred_element_type=jnp.float32).astype(jnp.bfloat16)
    queries = (query_base + jnp.dot(adapter_mid, adapter_up.T, preferred_element_type=jnp.float32)).astype(jnp.bfloat16)
    shaped = (GROUPS, REQ_DEV, NODES, HEADS, HEAD)
    cached = (GROUPS, REQ_DEV, HEADS, HEAD, CACHE)
    prompted = (GROUPS, HEADS, HEAD, PROMPT)

    def one_group(operands):
        return attend(operands[0], operands[1], operands[2], operands[3], operands[4], operands[5], operands[6], operands[7], operands[8])
    attended = lax.map(one_group, (queries.reshape(shaped), new_keys.reshape(shaped), new_values.reshape(shaped), prompt_keys.reshape(prompted), prompt_values.reshape(prompted), cache_keys.reshape(cached), cache_values.reshape(cached), cache_lengths.reshape(GROUPS, REQ_DEV), parents.reshape(GROUPS, REQ_DEV, NODES)))
    flattened = attended.reshape(TOKENS, HEADS * HEAD)
    return jnp.dot(flattened, out_weight, preferred_element_type=jnp.float32).astype(jnp.bfloat16)
```

```python
import math

import jax
import jax.numpy as jnp
from jax import lax
from jax.experimental import pallas as pl
from jax.experimental.pallas import tpu as pltpu
from jax.sharding import PartitionSpec as P

HEAD = 224
NT = (((1,), (1,)), ((), ()))
MESH = pl.DeviceIdType.MESH


def contract_rows(left, right):
    return lax.dot_general(left, right, NT, preferred_element_type=jnp.float32)


def ancestors(parents):
    node_count = parents.shape[1]
    columns = jnp.arange(node_count, dtype=jnp.int32)
    parent_hot = (parents[:, :, None] == columns[None, None, :]).astype(jnp.float32)
    reached = jnp.minimum(jnp.eye(node_count, dtype=jnp.float32)[None] + parent_hot, 1.0)
    reached = reached.astype(jnp.bfloat16)
    rounds = max(1, math.ceil(math.log2(node_count)))
    for sweep in range(rounds):
        step = jnp.einsum("rnm,rmk->rnk", reached, reached, preferred_element_type=jnp.float32)
        reached = jnp.minimum(reached.astype(jnp.float32) + step, 1.0).astype(jnp.bfloat16)
    return reached


def attend(queries, new_keys, new_values, prompt_k, prompt_v, cache_k, cache_v, lengths, reached):
    factor = 1.0 / math.sqrt(queries.shape[-1])
    s_prompt = (
        jnp.einsum("rnhe,hep->rnhp", queries, prompt_k, preferred_element_type=jnp.float32) * factor
    )
    s_cache = (
        jnp.einsum("rnhe,rhec->rnhc", queries, cache_k, preferred_element_type=jnp.float32) * factor
    )
    s_tree = (
        jnp.einsum("rnhe,rmhe->rnhm", queries, new_keys, preferred_element_type=jnp.float32)
        * factor
    )
    usable = jnp.arange(cache_k.shape[-1], dtype=jnp.int32)[None, :] < lengths[:, None]
    s_cache = jnp.where(usable[:, None, None, :], s_cache, -jnp.inf)
    s_tree = jnp.where(reached[:, :, None, :] > 0.5, s_tree, -jnp.inf)
    largest = jnp.maximum(
        jnp.maximum(
            jnp.max(s_prompt, axis=-1, keepdims=True), jnp.max(s_cache, axis=-1, keepdims=True)
        ),
        jnp.max(s_tree, axis=-1, keepdims=True),
    )
    e_prompt = jnp.exp(s_prompt - largest)
    e_cache = jnp.exp(s_cache - largest)
    e_tree = jnp.exp(s_tree - largest)
    totals = (
        jnp.sum(e_prompt, axis=-1, keepdims=True)
        + jnp.sum(e_cache, axis=-1, keepdims=True)
        + jnp.sum(e_tree, axis=-1, keepdims=True)
    )
    w_prompt = (e_prompt / totals).astype(jnp.bfloat16)
    w_cache = (e_cache / totals).astype(jnp.bfloat16)
    w_tree = (e_tree / totals).astype(jnp.bfloat16)
    result = jnp.einsum("rnhp,hep->rnhe", w_prompt, prompt_v, preferred_element_type=jnp.float32)
    result = result + jnp.einsum(
        "rnhc,rhec->rnhe", w_cache, cache_v, preferred_element_type=jnp.float32
    )
    result = result + jnp.einsum(
        "rnhm,rmhe->rnhe", w_tree, new_values, preferred_element_type=jnp.float32
    )
    return result.astype(jnp.bfloat16)


def remote(src, dst, send, recv, axis, index):
    return pltpu.make_async_remote_copy(
        src_ref=src,
        dst_ref=dst,
        send_sem=send,
        recv_sem=recv,
        device_id={axis: index},
        device_id_type=MESH,
    )


def line_position():
    h = lax.axis_index("gy")
    z = h // 2
    x = h - 2 * z
    return z, x


def greet_line(planes, z, x, extra):
    barrier = pltpu.get_barrier_semaphore()

    def signal(axis, index):
        pl.semaphore_signal(barrier, inc=1, device_id={axis: index}, device_id_type=MESH)

    signal("gy", 2 * z + 1 - x)
    for index in extra:
        signal("gx", index)

    @pl.when(z > 0)
    def _():
        signal("gy", 2 * (z - 1) + x)

    @pl.when(z < planes - 1)
    def _():
        signal("gy", 2 * (z + 1) + x)

    inner = jnp.where(z > 0, 1, 0) + jnp.where(z < planes - 1, 1, 0)
    pl.semaphore_wait(barrier, 1 + len(extra) + inner)


def pieces_of(rows):
    late = rows // 6
    half = (rows - late) // 2
    return ((0, half), (half, half), (2 * half, late))


def project_kernel(
    planes,
    x_ref,
    wq,
    wk,
    wv,
    wd,
    up,
    out,
    rows_buf,
    weights,
    part,
    core_in,
    y_out,
    y_in,
    w_sem,
    up_send,
    down_send,
    x_send,
    recv,
    c_send,
    c_recv,
    y_send,
    y_recv,
):
    z, x = line_position()
    mine = lax.axis_index("gx")
    y = mine // 2
    core = mine - 2 * y
    other_core = 2 * y + 1 - core
    other_y = 2 * (1 - y) + core
    shard = x_ref.shape[0]
    group_rows = 2 * shard
    ranges = pieces_of(shard)
    width = wq.shape[0]

    loads = []
    start = 0
    for slot, matrix in enumerate((wq, wk, wv, wd)):
        count = matrix.shape[0]
        load = pltpu.make_async_copy(
            matrix, weights.at[pl.ds(start, count)], w_sem.at[slot]
        )
        load.start()
        loads.append(load)
        start += count
    greet_line(planes, z, x, (other_core, other_y))

    def place(oz, ox, p):
        first, count = ranges[p]
        return rows_buf.at[pl.ds(pl.multiple_of((2 * oz + ox) * shard + first, 16), count)]

    def own(p):
        first, count = ranges[p]
        return x_ref.at[pl.ds(first, count)]

    def to_x(oz, ox, p, src):
        return remote(
            src, place(oz, ox, p), x_send.at[oz, p], recv.at[2 * oz + ox, p], "gy", 2 * z + 1 - x
        )

    def to_up(oz, ox, p, src):
        return remote(
            src,
            place(oz, ox, p),
            up_send.at[2 * oz + ox, p],
            recv.at[2 * oz + ox, p],
            "gy",
            2 * jnp.minimum(z + 1, planes - 1) + x,
        )

    def to_down(oz, ox, p, src):
        return remote(
            src,
            place(oz, ox, p),
            down_send.at[2 * oz + ox, p],
            recv.at[2 * oz + ox, p],
            "gy",
            2 * jnp.maximum(z - 1, 0) + x,
        )

    def arrived(oz, ox, p):
        ref = place(oz, ox, p)
        remote(ref, ref, x_send.at[0, 0], recv.at[2 * oz + ox, p], "gy", 2 * z + 1 - x).wait_recv()

    def both_ways(oz, ox, p, src):
        @pl.when(z < planes - 1)
        def _():
            to_up(oz, ox, p, src).start()

        @pl.when(z > 0)
        def _():
            to_down(oz, ox, p, src).start()

    to_x(z, x, 2, own(2)).start()
    for p in (0, 1, 2):
        both_ways(z, x, p, own(p))
        if p < 2:
            to_x(z, x, p, own(p)).start()
    rows_buf[pl.ds(pl.multiple_of((2 * z + x) * shard, 16), shard)] = x_ref[...]
    arrived(z, 1 - x, 2)
    both_ways(z, 1 - x, 2, place(z, 1 - x, 2))
    for load in loads:
        load.wait()

    def from_side(oz, below, p, ox):
        @pl.when(jnp.logical_and(oz >= 0, oz < planes))
        def _():
            arrived(oz, ox, p)
            src = place(oz, ox, p)
            if below:

                @pl.when(z < planes - 1)
                def _():
                    to_up(oz, ox, p, src).start()
            else:

                @pl.when(z > 0)
                def _():
                    to_down(oz, ox, p, src).start()

    def from_sides(distance, p, ox, cross):
        for below in (True, False):
            oz = z - distance if below else z + distance
            from_side(oz, below, p, ox)
            if cross:

                @pl.when(jnp.logical_and(oz >= 0, oz < planes))
                def _():
                    to_x(oz, x, p, place(oz, x, p)).start()

    def group_at(k):
        last = planes - 1
        low = jnp.where(z == 0, k, jnp.where(k == 0, 1, jnp.where(k == 1, 0, k)))
        m = last - z
        high = jnp.where(m == 0, k, jnp.where(k == 0, 1, jnp.where(k == 1, 0, k)))
        return jnp.where(z < 2, low, last - high)

    def core_copy(g):
        return remote(
            part.at[g], core_in.at[g // 2], c_send.at[g // 2], c_recv.at[g // 2], "gx", other_core
        )

    def y_copy():
        return remote(y_out, y_in, y_send.at[0], y_recv.at[0], "gx", other_y)

    def settle(g):
        @pl.when(g - 2 * (g // 2) == core)
        def _():
            core_copy(g).wait_recv()

            @pl.when(g // 2 != y)
            def _():
                y_out[...] = (part[g] + core_in[g // 2]).astype(y_out.dtype)
                y_copy().start()

    def step(k, carry):
        distance = k + 1
        for p in (0, 1):
            from_sides(distance, p, x, True)
        for ox in (x, 1 - x):
            from_sides(distance, 2, ox, False)

        @pl.when(k > 0)
        def _():
            settle(group_at(k - 1))

        g = group_at(k)
        for p in (0, 1):
            arrived(g, 1 - x, p)
        part[g] = lax.dot_general(
            weights[...],
            rows_buf[pl.ds(pl.multiple_of(g * group_rows, 16), group_rows)],
            NT,
            preferred_element_type=jnp.float32,
        )

        @pl.when(g - 2 * (g // 2) != core)
        def _():
            core_copy(g).start()

        return carry

    lax.fori_loop(0, planes, step, 0)
    settle(group_at(planes - 1))
    y_copy().wait_recv()
    total = part[mine] + core_in[mine // 2] + y_in[...].astype(jnp.float32)
    middle = total[3 * width :].astype(jnp.bfloat16)
    extra = jnp.dot(up[...], middle, preferred_element_type=jnp.float32)
    out[pl.ds(0, width)] = (total[:width] + extra).astype(jnp.bfloat16)
    out[pl.ds(width, 2 * width)] = total[width : 3 * width].astype(jnp.bfloat16)

    y_copy().wait_send()
    for half in range(planes // 2):
        core_copy(2 * half + 1 - core).wait_send()
    for oz in range(planes):
        for p in (0, 1):
            to_x(oz, x, p, place(oz, x, p)).wait_send()
        for ox in (0, 1):
            for p in (0, 1, 2):
                if p == 2:
                    sent = oz >= 0
                else:
                    sent = x == ox

                @pl.when(jnp.logical_and(sent, jnp.logical_and(oz <= z, z < planes - 1)))
                def _():
                    to_up(oz, ox, p, place(oz, ox, p)).wait_send()

                @pl.when(jnp.logical_and(sent, jnp.logical_and(oz >= z, z > 0)))
                def _():
                    to_down(oz, ox, p, place(oz, ox, p)).wait_send()

    to_x(z, x, 2, own(2)).wait_send()


def project(inputs, query_weight, key_weight, value_weight, adapter_down, adapter_up, planes):
    shard, columns = inputs.shape
    features = 3 * query_weight.shape[0] + adapter_down.shape[0]
    tokens = 2 * shard
    dma = pltpu.SemaphoreType.DMA
    vmem = pl.BlockSpec(memory_space=pltpu.VMEM)
    anywhere = pl.BlockSpec(memory_space=pl.ANY)

    def kernel(*refs):
        project_kernel(planes, *refs)

    return pl.pallas_call(
        kernel,
        out_shape=jax.ShapeDtypeStruct((3 * query_weight.shape[0], tokens), jnp.bfloat16),
        in_specs=[vmem, anywhere, anywhere, anywhere, anywhere, vmem],
        out_specs=vmem,
        scratch_shapes=[
            pltpu.VMEM((planes * tokens, columns), jnp.bfloat16),
            pltpu.VMEM((features, columns), jnp.bfloat16),
            pltpu.VMEM((planes, features, tokens), jnp.float32),
            pltpu.VMEM((planes // 2, features, tokens), jnp.float32),
            pltpu.VMEM((features, tokens), jnp.bfloat16),
            pltpu.VMEM((features, tokens), jnp.bfloat16),
            dma((4,)),
            dma((2 * planes, 3)),
            dma((2 * planes, 3)),
            dma((planes, 3)),
            dma((2 * planes, 3)),
            dma((planes // 2,)),
            dma((planes // 2,)),
            dma((1,)),
            dma((1,)),
        ],
        compiler_params=pltpu.CompilerParams(
            collective_id=0, has_side_effects=True, vmem_limit_bytes=44 * 1024 * 1024
        ),
        cost_estimate=pl.CostEstimate(
            flops=2 * planes * tokens * columns * features,
            bytes_accessed=2 * (planes * tokens + features) * columns,
            transcendentals=0,
        ),
    )(inputs, query_weight, key_weight, value_weight, adapter_down, adapter_up)


def output_kernel(
    planes,
    att,
    weight,
    out,
    x_out,
    x_in,
    kept,
    z_out,
    up_in,
    down_in,
    x_send,
    x_recv,
    z_send,
    up_recv,
    down_recv,
):
    z, x = line_position()
    block = out.shape[0]
    greet_line(planes, z, x, ())

    def partial(oz, ox):
        rows = weight[pl.ds(pl.multiple_of((2 * oz + ox) * block, 16), block)]
        return lax.dot_general(rows, att[...], NT, preferred_element_type=jnp.float32)

    def plane_at(k):
        last = planes - 1
        low = jnp.where(z == 0, last - k, jnp.where(k == 0, 3, jnp.where(k == 1, 0, 3 - k + 1)))
        low = jnp.where(jnp.logical_and(z == 1, k == 3), 1, low)
        m = last - z
        high = jnp.where(m == 0, last - k, jnp.where(k == 0, 3, jnp.where(k == 1, 0, 3 - k + 1)))
        high = jnp.where(jnp.logical_and(m == 1, k == 3), 1, high)
        return jnp.where(z < 2, low, last - high)

    def x_copy(oz):
        return remote(
            x_out.at[oz], x_in.at[oz], x_send.at[oz], x_recv.at[oz], "gy", 2 * z + 1 - x
        )

    def up_copy(oz):
        return remote(
            z_out.at[oz],
            up_in.at[oz],
            z_send.at[oz],
            up_recv.at[oz],
            "gy",
            2 * jnp.minimum(z + 1, planes - 1) + x,
        )

    def down_copy(oz):
        return remote(
            z_out.at[oz],
            down_in.at[oz],
            z_send.at[oz],
            down_recv.at[oz],
            "gy",
            2 * jnp.maximum(z - 1, 0) + x,
        )

    def cross(k, carry):
        oz = plane_at(k)
        x_out[oz] = partial(oz, 1 - x).astype(x_out.dtype)
        x_copy(oz).start()
        return carry

    lax.fori_loop(0, planes, cross, 0)

    def keep(k, carry):
        kept[k] = partial(k, x)
        return carry

    lax.fori_loop(0, planes, keep, 0)

    def along(k, carry):
        oz = plane_at(k)
        x_copy(oz).wait_recv()
        kept[oz] = kept[oz] + x_in[oz].astype(jnp.float32)

        @pl.when(jnp.logical_and(z > 0, oz >= z))
        def _():
            up_copy(oz).wait_recv()
            kept[oz] = kept[oz] + up_in[oz].astype(jnp.float32)

        @pl.when(jnp.logical_and(z < planes - 1, oz <= z))
        def _():
            down_copy(oz).wait_recv()
            kept[oz] = kept[oz] + down_in[oz].astype(jnp.float32)

        @pl.when(oz > z)
        def _():
            z_out[oz] = kept[oz].astype(z_out.dtype)
            up_copy(oz).start()

        @pl.when(oz < z)
        def _():
            z_out[oz] = kept[oz].astype(z_out.dtype)
            down_copy(oz).start()

        return carry

    lax.fori_loop(0, planes, along, 0)
    out[...] = kept[z].astype(out.dtype)

    def finish(oz, carry):
        x_copy(oz).wait_send()

        @pl.when(oz != z)
        def _():
            up_copy(oz).wait_send()

        return carry

    lax.fori_loop(0, planes, finish, 0)


def project_out(att, weight, planes):
    tokens = att.shape[0]
    block = weight.shape[0] // (2 * planes)
    dma = pltpu.SemaphoreType.DMA
    vmem = pl.BlockSpec(memory_space=pltpu.VMEM)
    blocks = (planes, block, tokens)

    def kernel(*refs):
        output_kernel(planes, *refs)

    return pl.pallas_call(
        kernel,
        out_shape=jax.ShapeDtypeStruct((block, tokens), jnp.bfloat16),
        in_specs=[vmem, vmem],
        out_specs=vmem,
        scratch_shapes=[
            pltpu.VMEM(blocks, jnp.bfloat16),
            pltpu.VMEM(blocks, jnp.bfloat16),
            pltpu.VMEM(blocks, jnp.float32),
            pltpu.VMEM(blocks, jnp.bfloat16),
            pltpu.VMEM(blocks, jnp.bfloat16),
            pltpu.VMEM(blocks, jnp.bfloat16),
            dma((planes,)),
            dma((planes,)),
            dma((planes,)),
            dma((planes,)),
            dma((planes,)),
        ],
        compiler_params=pltpu.CompilerParams(
            collective_id=1, has_side_effects=True, vmem_limit_bytes=32 * 1024 * 1024
        ),
    )(att, weight)


def per_device(
    inputs,
    query_weight,
    key_weight,
    value_weight,
    adapter_down,
    adapter_up,
    prompt_keys,
    prompt_values,
    cache_keys,
    cache_values,
    cache_lengths,
    parents,
    out_weight,
):
    requests = cache_keys.shape[0]
    node_count = parents.shape[1]
    local_rows = requests * node_count
    head_width = query_weight.shape[0]
    head_count = head_width // HEAD
    lines = lax.axis_size("gx") == 4 and lax.axis_size("gy") == 8
    shaped = (requests, node_count, head_count, HEAD)
    cached = (requests, head_count, HEAD, cache_keys.shape[2])
    reached = ancestors(parents)
    if lines:
        planes = lax.axis_size("gy") // 2
        gathered_weight = lax.all_gather(out_weight.T, "gx", axis=0, tiled=True)
        projected = project(
            inputs, query_weight, key_weight, value_weight, adapter_down, adapter_up, planes
        )
        queries = projected[:head_width].T
        new_keys = projected[head_width : 2 * head_width].T
        new_values = projected[2 * head_width :].T
    else:
        all_rows = lax.all_gather(inputs, "gy", axis=0, tiled=True)
        mixture = lax.psum_scatter(
            jnp.concatenate(
                [
                    contract_rows(all_rows, matrix)
                    for matrix in (query_weight, key_weight, value_weight, adapter_down)
                ],
                axis=1,
            ),
            "gx",
            scatter_dimension=0,
            tiled=True,
        )
        query_base = mixture[:, :head_width]
        new_keys = mixture[:, head_width : 2 * head_width].astype(jnp.bfloat16)
        new_values = mixture[:, 2 * head_width : 3 * head_width].astype(jnp.bfloat16)
        adapter_mid = mixture[:, 3 * head_width :].astype(jnp.bfloat16)
        queries = (query_base + contract_rows(adapter_mid, adapter_up)).astype(jnp.bfloat16)
    attended = attend(
        queries.reshape(shaped),
        new_keys.reshape(shaped),
        new_values.reshape(shaped),
        prompt_keys,
        prompt_values,
        cache_keys.reshape(cached),
        cache_values.reshape(cached),
        cache_lengths,
        reached,
    )
    flattened = attended.reshape(local_rows, head_width)
    if lines:
        return project_out(flattened, gathered_weight, planes).T
    partial_sums = jnp.dot(
        flattened,
        lax.all_gather(out_weight, "gx", axis=1, tiled=True),
        preferred_element_type=jnp.float32,
    )
    return lax.psum_scatter(
        partial_sums.astype(jnp.bfloat16), "gy", scatter_dimension=1, tiled=True
    )


def solution(mesh):
    placed = (
        P("gy", "gx"),
        P("gy", "gx"),
        P("gy", "gx"),
        P("gy", "gx"),
        P(None, "gx"),
        P("gy", None),
        P("gx", "gy", None),
        P("gx", "gy", None),
        P("gx", "gy", None),
        P("gx", "gy", None),
        P("gx"),
        P("gx", None),
        P("gy", "gx"),
    )
    return jax.shard_map(
        per_device, mesh=mesh, in_specs=placed, out_specs=P("gx", "gy"), check_vma=False
    )
```

```python
import math

import jax
import jax.numpy as jnp
from jax import lax
from jax.experimental import pallas as pl
from jax.experimental.pallas import tpu as pltpu
from jax.sharding import PartitionSpec as P

HEAD = 224
NT = (((1,), (1,)), ((), ()))
MESH = pl.DeviceIdType.MESH


def contract_rows(left, right):
    return lax.dot_general(left, right, NT, preferred_element_type=jnp.float32)


def ancestors(parents):
    node_count = parents.shape[1]
    columns = jnp.arange(node_count, dtype=jnp.int32)
    parent_hot = (parents[:, :, None] == columns[None, None, :]).astype(jnp.float32)
    reached = jnp.minimum(jnp.eye(node_count, dtype=jnp.float32)[None] + parent_hot, 1.0)
    reached = reached.astype(jnp.bfloat16)
    rounds = max(1, math.ceil(math.log2(node_count)))
    for sweep in range(rounds):
        step = jnp.einsum("rnm,rmk->rnk", reached, reached, preferred_element_type=jnp.float32)
        reached = jnp.minimum(reached.astype(jnp.float32) + step, 1.0).astype(jnp.bfloat16)
    return reached


def attend(queries, new_keys, new_values, prompt_k, prompt_v, cache_k, cache_v, lengths, reached):
    factor = 1.0 / math.sqrt(queries.shape[-1])
    s_prompt = (
        jnp.einsum("rnhe,hep->rnhp", queries, prompt_k, preferred_element_type=jnp.float32) * factor
    )
    s_cache = (
        jnp.einsum("rnhe,rhec->rnhc", queries, cache_k, preferred_element_type=jnp.float32) * factor
    )
    s_tree = (
        jnp.einsum("rnhe,rmhe->rnhm", queries, new_keys, preferred_element_type=jnp.float32)
        * factor
    )
    usable = jnp.arange(cache_k.shape[-1], dtype=jnp.int32)[None, :] < lengths[:, None]
    s_cache = jnp.where(usable[:, None, None, :], s_cache, -jnp.inf)
    s_tree = jnp.where(reached[:, :, None, :] > 0.5, s_tree, -jnp.inf)
    largest = jnp.maximum(
        jnp.maximum(
            jnp.max(s_prompt, axis=-1, keepdims=True), jnp.max(s_cache, axis=-1, keepdims=True)
        ),
        jnp.max(s_tree, axis=-1, keepdims=True),
    )
    e_prompt = jnp.exp(s_prompt - largest)
    e_cache = jnp.exp(s_cache - largest)
    e_tree = jnp.exp(s_tree - largest)
    totals = (
        jnp.sum(e_prompt, axis=-1, keepdims=True)
        + jnp.sum(e_cache, axis=-1, keepdims=True)
        + jnp.sum(e_tree, axis=-1, keepdims=True)
    )
    w_prompt = (e_prompt / totals).astype(jnp.bfloat16)
    w_cache = (e_cache / totals).astype(jnp.bfloat16)
    w_tree = (e_tree / totals).astype(jnp.bfloat16)
    result = jnp.einsum("rnhp,hep->rnhe", w_prompt, prompt_v, preferred_element_type=jnp.float32)
    result = result + jnp.einsum(
        "rnhc,rhec->rnhe", w_cache, cache_v, preferred_element_type=jnp.float32
    )
    result = result + jnp.einsum(
        "rnhm,rmhe->rnhe", w_tree, new_values, preferred_element_type=jnp.float32
    )
    return result.astype(jnp.bfloat16)


def remote(src, dst, send, recv, axis, index):
    return pltpu.make_async_remote_copy(
        src_ref=src,
        dst_ref=dst,
        send_sem=send,
        recv_sem=recv,
        device_id={axis: index},
        device_id_type=MESH,
    )


def line_position():
    h = lax.axis_index("gy")
    z = h // 2
    x = h - 2 * z
    return z, x


def greet_line(planes, z, x, extra):
    barrier = pltpu.get_barrier_semaphore()

    def signal(axis, index):
        pl.semaphore_signal(barrier, inc=1, device_id={axis: index}, device_id_type=MESH)

    signal("gy", 2 * z + 1 - x)
    for index in extra:
        signal("gx", index)

    @pl.when(z > 0)
    def _():
        signal("gy", 2 * (z - 1) + x)

    @pl.when(z < planes - 1)
    def _():
        signal("gy", 2 * (z + 1) + x)

    inner = jnp.where(z > 0, 1, 0) + jnp.where(z < planes - 1, 1, 0)
    pl.semaphore_wait(barrier, 1 + len(extra) + inner)


def pieces_of(rows):
    late = rows // 6
    half = (rows - late) // 2
    return ((0, half), (half, half), (2 * half, late))


def project_kernel(
    planes,
    x_ref,
    wq,
    wk,
    wv,
    wd,
    up,
    out,
    rows_buf,
    weights,
    part,
    core_in,
    y_out,
    y_in,
    w_sem,
    up_send,
    down_send,
    x_send,
    recv,
    c_send,
    c_recv,
    y_send,
    y_recv,
):
    z, x = line_position()
    mine = lax.axis_index("gx")
    y = mine // 2
    core = mine - 2 * y
    other_core = 2 * y + 1 - core
    other_y = 2 * (1 - y) + core
    shard = x_ref.shape[0]
    group_rows = 2 * shard
    ranges = pieces_of(shard)
    width = wq.shape[0]

    loads = []
    start = 0
    for slot, matrix in enumerate((wq, wk, wv, wd)):
        count = matrix.shape[0]
        load = pltpu.make_async_copy(
            matrix, weights.at[pl.ds(start, count)], w_sem.at[slot]
        )
        load.start()
        loads.append(load)
        start += count
    greet_line(planes, z, x, (other_core, other_y))

    def place(oz, ox, p):
        first, count = ranges[p]
        return rows_buf.at[pl.ds(pl.multiple_of((2 * oz + ox) * shard + first, 16), count)]

    def own(p):
        first, count = ranges[p]
        return x_ref.at[pl.ds(first, count)]

    def to_x(oz, ox, p, src):
        return remote(
            src, place(oz, ox, p), x_send.at[oz, p], recv.at[2 * oz + ox, p], "gy", 2 * z + 1 - x
        )

    def to_up(oz, ox, p, src):
        return remote(
            src,
            place(oz, ox, p),
            up_send.at[2 * oz + ox, p],
            recv.at[2 * oz + ox, p],
            "gy",
            2 * jnp.minimum(z + 1, planes - 1) + x,
        )

    def to_down(oz, ox, p, src):
        return remote(
            src,
            place(oz, ox, p),
            down_send.at[2 * oz + ox, p],
            recv.at[2 * oz + ox, p],
            "gy",
            2 * jnp.maximum(z - 1, 0) + x,
        )

    def arrived(oz, ox, p):
        ref = place(oz, ox, p)
        remote(ref, ref, x_send.at[0, 0], recv.at[2 * oz + ox, p], "gy", 2 * z + 1 - x).wait_recv()

    def both_ways(oz, ox, p, src):
        @pl.when(z < planes - 1)
        def _():
            to_up(oz, ox, p, src).start()

        @pl.when(z > 0)
        def _():
            to_down(oz, ox, p, src).start()

    to_x(z, x, 2, own(2)).start()
    for p in (0, 1, 2):
        both_ways(z, x, p, own(p))
        if p < 2:
            to_x(z, x, p, own(p)).start()
    mine_copy = pltpu.make_async_copy(
        x_ref, rows_buf.at[pl.ds(pl.multiple_of((2 * z + x) * shard, 16), shard)], w_sem.at[4]
    )
    mine_copy.start()
    arrived(z, 1 - x, 2)
    both_ways(z, 1 - x, 2, place(z, 1 - x, 2))
    for load in loads:
        load.wait()
    mine_copy.wait()

    def from_side(oz, below, p, ox):
        @pl.when(jnp.logical_and(oz >= 0, oz < planes))
        def _():
            arrived(oz, ox, p)
            src = place(oz, ox, p)
            if below:

                @pl.when(z < planes - 1)
                def _():
                    to_up(oz, ox, p, src).start()
            else:

                @pl.when(z > 0)
                def _():
                    to_down(oz, ox, p, src).start()

    def from_sides(distance, p, ox, cross):
        for below in (True, False):
            oz = z - distance if below else z + distance
            from_side(oz, below, p, ox)
            if cross:

                @pl.when(jnp.logical_and(oz >= 0, oz < planes))
                def _():
                    to_x(oz, x, p, place(oz, x, p)).start()

    def group_at(k):
        last = planes - 1
        low = jnp.where(z == 0, k, jnp.where(k == 0, 1, jnp.where(k == 1, 0, k)))
        m = last - z
        high = jnp.where(m == 0, k, jnp.where(k == 0, 1, jnp.where(k == 1, 0, k)))
        return jnp.where(z < 2, low, last - high)

    def core_copy(g):
        return remote(
            part.at[g], core_in.at[g // 2], c_send.at[g // 2], c_recv.at[g // 2], "gx", other_core
        )

    def y_copy():
        return remote(y_out, y_in, y_send.at[0], y_recv.at[0], "gx", other_y)

    def settle(g):
        @pl.when(g - 2 * (g // 2) == core)
        def _():
            core_copy(g).wait_recv()

            @pl.when(g // 2 != y)
            def _():
                y_out[...] = (part[g] + core_in[g // 2]).astype(y_out.dtype)
                y_copy().start()

    def step(k, carry):
        distance = k + 1
        for p in (0, 1):
            from_sides(distance, p, x, True)
        for ox in (x, 1 - x):
            from_sides(distance, 2, ox, False)

        @pl.when(k > 0)
        def _():
            settle(group_at(k - 1))

        g = group_at(k)
        for p in (0, 1):
            arrived(g, 1 - x, p)
        part[g] = lax.dot_general(
            weights[...],
            rows_buf[pl.ds(pl.multiple_of(g * group_rows, 16), group_rows)],
            NT,
            preferred_element_type=jnp.float32,
        )

        @pl.when(g - 2 * (g // 2) != core)
        def _():
            core_copy(g).start()

        return carry

    lax.fori_loop(0, planes, step, 0)
    settle(group_at(planes - 1))
    y_copy().wait_recv()
    total = part[mine] + core_in[mine // 2] + y_in[...].astype(jnp.float32)
    middle = total[3 * width :].astype(jnp.bfloat16)
    extra = jnp.dot(up[...], middle, preferred_element_type=jnp.float32)
    out[pl.ds(0, width)] = (total[:width] + extra).astype(jnp.bfloat16)
    out[pl.ds(width, 2 * width)] = total[width : 3 * width].astype(jnp.bfloat16)

    y_copy().wait_send()
    for half in range(planes // 2):
        core_copy(2 * half + 1 - core).wait_send()
    for oz in range(planes):
        for p in (0, 1):
            to_x(oz, x, p, place(oz, x, p)).wait_send()
        for ox in (0, 1):
            for p in (0, 1, 2):
                if p == 2:
                    sent = oz >= 0
                else:
                    sent = x == ox

                @pl.when(jnp.logical_and(sent, jnp.logical_and(oz <= z, z < planes - 1)))
                def _():
                    to_up(oz, ox, p, place(oz, ox, p)).wait_send()

                @pl.when(jnp.logical_and(sent, jnp.logical_and(oz >= z, z > 0)))
                def _():
                    to_down(oz, ox, p, place(oz, ox, p)).wait_send()

    to_x(z, x, 2, own(2)).wait_send()


def project(inputs, query_weight, key_weight, value_weight, adapter_down, adapter_up, planes):
    shard, columns = inputs.shape
    features = 3 * query_weight.shape[0] + adapter_down.shape[0]
    tokens = 2 * shard
    dma = pltpu.SemaphoreType.DMA
    vmem = pl.BlockSpec(memory_space=pltpu.VMEM)
    anywhere = pl.BlockSpec(memory_space=pl.ANY)

    def kernel(*refs):
        project_kernel(planes, *refs)

    return pl.pallas_call(
        kernel,
        out_shape=jax.ShapeDtypeStruct((3 * query_weight.shape[0], tokens), jnp.bfloat16),
        in_specs=[anywhere, anywhere, anywhere, anywhere, anywhere, vmem],
        out_specs=vmem,
        scratch_shapes=[
            pltpu.VMEM((planes * tokens, columns), jnp.bfloat16),
            pltpu.VMEM((features, columns), jnp.bfloat16),
            pltpu.VMEM((planes, features, tokens), jnp.float32),
            pltpu.VMEM((planes // 2, features, tokens), jnp.float32),
            pltpu.VMEM((features, tokens), jnp.bfloat16),
            pltpu.VMEM((features, tokens), jnp.bfloat16),
            dma((5,)),
            dma((2 * planes, 3)),
            dma((2 * planes, 3)),
            dma((planes, 3)),
            dma((2 * planes, 3)),
            dma((planes // 2,)),
            dma((planes // 2,)),
            dma((1,)),
            dma((1,)),
        ],
        compiler_params=pltpu.CompilerParams(
            collective_id=0, has_side_effects=True, vmem_limit_bytes=60 * 1024 * 1024
        ),
        cost_estimate=pl.CostEstimate(
            flops=2 * planes * tokens * columns * features,
            bytes_accessed=2 * (planes * tokens + features) * columns,
            transcendentals=0,
        ),
    )(inputs, query_weight, key_weight, value_weight, adapter_down, adapter_up)


def gather_kernel(planes, att, out, local_sem, up_send, down_send, x_send, recv):
    z, x = line_position()
    tokens = att.shape[0]
    late = tokens // 6 // 16 * 16
    ranges = ((0, tokens - late), (tokens - late, late))
    local = pltpu.make_async_copy(att, out.at[2 * z + x], local_sem.at[0])
    local.start()
    greet_line(planes, z, x, ())

    def place(oz, ox, p):
        first, count = ranges[p]
        return out.at[2 * oz + ox, pl.ds(first, count)]

    def own(p):
        first, count = ranges[p]
        return att.at[pl.ds(first, count)]

    def to_x(oz, ox, p, src):
        return remote(
            src, place(oz, ox, p), x_send.at[oz, p], recv.at[2 * oz + ox, p], "gy", 2 * z + 1 - x
        )

    def to_up(oz, ox, p, src):
        return remote(
            src,
            place(oz, ox, p),
            up_send.at[2 * oz + ox, p],
            recv.at[2 * oz + ox, p],
            "gy",
            2 * jnp.minimum(z + 1, planes - 1) + x,
        )

    def to_down(oz, ox, p, src):
        return remote(
            src,
            place(oz, ox, p),
            down_send.at[2 * oz + ox, p],
            recv.at[2 * oz + ox, p],
            "gy",
            2 * jnp.maximum(z - 1, 0) + x,
        )

    def arrived(oz, ox, p):
        ref = place(oz, ox, p)
        remote(ref, ref, x_send.at[0, 0], recv.at[2 * oz + ox, p], "gy", 2 * z + 1 - x).wait_recv()

    def both_ways(oz, ox, p, src):
        @pl.when(z < planes - 1)
        def _():
            to_up(oz, ox, p, src).start()

        @pl.when(z > 0)
        def _():
            to_down(oz, ox, p, src).start()

    to_x(z, x, 1, own(1)).start()
    for p in (0, 1):
        both_ways(z, x, p, own(p))
    to_x(z, x, 0, own(0)).start()
    arrived(z, 1 - x, 1)
    both_ways(z, 1 - x, 1, place(z, 1 - x, 1))

    def step(k, carry):
        for p, same in ((0, True), (1, True), (1, False)):
            ox = x if same else 1 - x
            for below in (True, False):
                oz = z - (k + 1) if below else z + (k + 1)

                @pl.when(jnp.logical_and(oz >= 0, oz < planes))
                def _():
                    arrived(oz, ox, p)
                    src = place(oz, ox, p)
                    if below:

                        @pl.when(z < planes - 1)
                        def _():
                            to_up(oz, ox, p, src).start()
                    else:

                        @pl.when(z > 0)
                        def _():
                            to_down(oz, ox, p, src).start()

                    if p == 0:
                        to_x(oz, ox, p, src).start()

        return carry

    lax.fori_loop(0, planes - 1, step, 0)
    local.wait()
    for oz in range(planes):
        arrived(oz, 1 - x, 0)
        to_x(oz, x, 0, place(oz, x, 0)).wait_send()
        for ox in (0, 1):
            for p in (0, 1):
                sent = oz >= 0 if p == 1 else x == ox

                @pl.when(jnp.logical_and(sent, jnp.logical_and(oz <= z, z < planes - 1)))
                def _():
                    to_up(oz, ox, p, place(oz, ox, p)).wait_send()

                @pl.when(jnp.logical_and(sent, jnp.logical_and(oz >= z, z > 0)))
                def _():
                    to_down(oz, ox, p, place(oz, ox, p)).wait_send()

    to_x(z, x, 1, own(1)).wait_send()


def gather_heads(att, planes):
    dma = pltpu.SemaphoreType.DMA
    vmem = pl.BlockSpec(memory_space=pltpu.VMEM)

    def kernel(*refs):
        gather_kernel(planes, *refs)

    return pl.pallas_call(
        kernel,
        out_shape=jax.ShapeDtypeStruct((2 * planes,) + att.shape, jnp.bfloat16),
        in_specs=[vmem],
        out_specs=vmem,
        scratch_shapes=[
            dma((1,)),
            dma((2 * planes, 2)),
            dma((2 * planes, 2)),
            dma((planes, 2)),
            dma((2 * planes, 2)),
        ],
        compiler_params=pltpu.CompilerParams(
            collective_id=1, has_side_effects=True, vmem_limit_bytes=16 * 1024 * 1024
        ),
    )(att)


def column_block(out_weight):
    across = lax.axis_size("gx")
    heads = lax.axis_size("gy")
    height, width = out_weight.shape
    cut = out_weight.reshape(across, height // across, 2, width // 2)
    cut = cut.transpose(0, 2, 1, 3).reshape(heads, height // across, width // 2)
    h = lax.axis_index("gy")
    target = 2 * lax.axis_index("gx") + lax.rem(h, 2)
    got = []
    for p in range(heads):
        moves = [
            (g * heads + k, ((k ^ p) // 2) * heads + 2 * g + (k ^ p) % 2)
            for g in range(across)
            for k in range(heads)
        ]
        piece = lax.dynamic_index_in_dim(cut, h ^ p, keepdims=False)
        got.append(lax.ppermute(piece, ("gx", "gy"), moves))
    mixed = jnp.stack(got)
    order = jnp.arange(heads, dtype=jnp.int32) ^ target
    sorted_heads = jnp.take(mixed, order, axis=0)
    return lax.all_gather(sorted_heads, "gx", axis=1, tiled=True)


def per_device(
    inputs,
    query_weight,
    key_weight,
    value_weight,
    adapter_down,
    adapter_up,
    prompt_keys,
    prompt_values,
    cache_keys,
    cache_values,
    cache_lengths,
    parents,
    out_weight,
):
    requests = cache_keys.shape[0]
    node_count = parents.shape[1]
    local_rows = requests * node_count
    head_width = query_weight.shape[0]
    head_count = head_width // HEAD
    lines = lax.axis_size("gx") == 4 and lax.axis_size("gy") == 8
    shaped = (requests, node_count, head_count, HEAD)
    cached = (requests, head_count, HEAD, cache_keys.shape[2])
    reached = ancestors(parents)
    if lines:
        planes = lax.axis_size("gy") // 2
        columns = column_block(out_weight)
        projected = project(
            inputs, query_weight, key_weight, value_weight, adapter_down, adapter_up, planes
        )
        queries = projected[:head_width].T
        new_keys = projected[head_width : 2 * head_width].T
        new_values = projected[2 * head_width :].T
    else:
        all_rows = lax.all_gather(inputs, "gy", axis=0, tiled=True)
        mixture = lax.psum_scatter(
            jnp.concatenate(
                [
                    contract_rows(all_rows, matrix)
                    for matrix in (query_weight, key_weight, value_weight, adapter_down)
                ],
                axis=1,
            ),
            "gx",
            scatter_dimension=0,
            tiled=True,
        )
        query_base = mixture[:, :head_width]
        new_keys = mixture[:, head_width : 2 * head_width].astype(jnp.bfloat16)
        new_values = mixture[:, 2 * head_width : 3 * head_width].astype(jnp.bfloat16)
        adapter_mid = mixture[:, 3 * head_width :].astype(jnp.bfloat16)
        queries = (query_base + contract_rows(adapter_mid, adapter_up)).astype(jnp.bfloat16)
    attended = attend(
        queries.reshape(shaped),
        new_keys.reshape(shaped),
        new_values.reshape(shaped),
        prompt_keys,
        prompt_values,
        cache_keys.reshape(cached),
        cache_values.reshape(cached),
        cache_lengths,
        reached,
    )
    flattened = attended.reshape(local_rows, head_width)
    if lines:
        everyone = gather_heads(flattened, planes)
        return jnp.einsum(
            "hre,hec->rc", everyone, columns, preferred_element_type=jnp.float32
        ).astype(jnp.bfloat16)
    partial_sums = jnp.dot(
        flattened,
        lax.all_gather(out_weight, "gx", axis=1, tiled=True),
        preferred_element_type=jnp.float32,
    )
    return lax.psum_scatter(
        partial_sums.astype(jnp.bfloat16), "gy", scatter_dimension=1, tiled=True
    )


def solution(mesh):
    placed = (
        P("gy", "gx"),
        P("gy", "gx"),
        P("gy", "gx"),
        P("gy", "gx"),
        P(None, "gx"),
        P("gy", None),
        P("gx", "gy", None),
        P("gx", "gy", None),
        P("gx", "gy", None),
        P("gx", "gy", None),
        P("gx"),
        P("gx", None),
        P("gy", "gx"),
    )
    return jax.shard_map(
        per_device, mesh=mesh, in_specs=placed, out_specs=P("gx", "gy"), check_vma=False
    )
```

```python
import math

import jax
import jax.numpy as jnp
from jax import lax
from jax.experimental import pallas as pl
from jax.experimental.pallas import tpu as pltpu
from jax.sharding import PartitionSpec as P

HEAD = 224
NT = (((1,), (1,)), ((), ()))
MESH = pl.DeviceIdType.MESH


def contract_rows(left, right):
    return lax.dot_general(left, right, NT, preferred_element_type=jnp.float32)


def ancestors(parents):
    node_count = parents.shape[1]
    columns = jnp.arange(node_count, dtype=jnp.int32)
    parent_hot = (parents[:, :, None] == columns[None, None, :]).astype(jnp.float32)
    reached = jnp.minimum(jnp.eye(node_count, dtype=jnp.float32)[None] + parent_hot, 1.0)
    reached = reached.astype(jnp.bfloat16)
    rounds = max(1, math.ceil(math.log2(node_count)))
    for sweep in range(rounds):
        step = jnp.einsum("rnm,rmk->rnk", reached, reached, preferred_element_type=jnp.float32)
        reached = jnp.minimum(reached.astype(jnp.float32) + step, 1.0).astype(jnp.bfloat16)
    return reached


def attend(queries, new_keys, new_values, prompt_k, prompt_v, cache_k, cache_v, lengths, reached):
    factor = 1.0 / math.sqrt(queries.shape[-1])
    s_prompt = (
        jnp.einsum("rnhe,hep->rnhp", queries, prompt_k, preferred_element_type=jnp.float32) * factor
    )
    s_cache = (
        jnp.einsum("rnhe,rhec->rnhc", queries, cache_k, preferred_element_type=jnp.float32) * factor
    )
    s_tree = (
        jnp.einsum("rnhe,rmhe->rnhm", queries, new_keys, preferred_element_type=jnp.float32)
        * factor
    )
    usable = jnp.arange(cache_k.shape[-1], dtype=jnp.int32)[None, :] < lengths[:, None]
    s_cache = jnp.where(usable[:, None, None, :], s_cache, -jnp.inf)
    s_tree = jnp.where(reached[:, :, None, :] > 0.5, s_tree, -jnp.inf)
    largest = jnp.maximum(
        jnp.maximum(
            jnp.max(s_prompt, axis=-1, keepdims=True), jnp.max(s_cache, axis=-1, keepdims=True)
        ),
        jnp.max(s_tree, axis=-1, keepdims=True),
    )
    e_prompt = jnp.exp(s_prompt - largest)
    e_cache = jnp.exp(s_cache - largest)
    e_tree = jnp.exp(s_tree - largest)
    totals = (
        jnp.sum(e_prompt, axis=-1, keepdims=True)
        + jnp.sum(e_cache, axis=-1, keepdims=True)
        + jnp.sum(e_tree, axis=-1, keepdims=True)
    )
    w_prompt = (e_prompt / totals).astype(jnp.bfloat16)
    w_cache = (e_cache / totals).astype(jnp.bfloat16)
    w_tree = (e_tree / totals).astype(jnp.bfloat16)
    result = jnp.einsum("rnhp,hep->rnhe", w_prompt, prompt_v, preferred_element_type=jnp.float32)
    result = result + jnp.einsum(
        "rnhc,rhec->rnhe", w_cache, cache_v, preferred_element_type=jnp.float32
    )
    result = result + jnp.einsum(
        "rnhm,rmhe->rnhe", w_tree, new_values, preferred_element_type=jnp.float32
    )
    return result.astype(jnp.bfloat16)


def remote(src, dst, send, recv, axis, index):
    return pltpu.make_async_remote_copy(
        src_ref=src,
        dst_ref=dst,
        send_sem=send,
        recv_sem=recv,
        device_id={axis: index},
        device_id_type=MESH,
    )


def line_position():
    h = lax.axis_index("gy")
    z = h // 2
    x = h - 2 * z
    return z, x


def greet_line(planes, z, x, extra, more=0):
    barrier = pltpu.get_barrier_semaphore()

    def signal(axis, index):
        pl.semaphore_signal(barrier, inc=1, device_id={axis: index}, device_id_type=MESH)

    signal("gy", 2 * z + 1 - x)
    for index in extra:
        signal("gx", index)

    @pl.when(z > 0)
    def _():
        signal("gy", 2 * (z - 1) + x)

    @pl.when(z < planes - 1)
    def _():
        signal("gy", 2 * (z + 1) + x)

    inner = jnp.where(z > 0, 1, 0) + jnp.where(z < planes - 1, 1, 0)
    pl.semaphore_wait(barrier, 1 + len(extra) + inner + more)


def pieces_of(rows):
    late = rows // 6
    half = (rows - late) // 2
    return ((0, half), (half, half), (2 * half, late))


def project_kernel(
    planes,
    x_ref,
    wq,
    wk,
    wv,
    wd,
    up,
    wo,
    out,
    cols,
    halves,
    o_send,
    o_recv,
    spread_send,
    spread_recv,
    rows_buf,
    weights,
    part,
    core_in,
    y_out,
    y_in,
    w_sem,
    up_send,
    down_send,
    x_send,
    recv,
    c_send,
    c_recv,
    y_send,
    y_recv,
):
    z, x = line_position()
    mine = lax.axis_index("gx")
    y = mine // 2
    core = mine - 2 * y
    other_core = 2 * y + 1 - core
    other_y = 2 * (1 - y) + core
    shard = x_ref.shape[0]
    group_rows = 2 * shard
    ranges = pieces_of(shard)
    width = wq.shape[0]

    loads = []
    start = 0
    for slot, matrix in enumerate((wq, wk, wv, wd)):
        count = matrix.shape[0]
        load = pltpu.make_async_copy(
            matrix, weights.at[pl.ds(start, count)], w_sem.at[slot]
        )
        load.start()
        loads.append(load)
        start += count

    gets = core == z - 2 * (z // 2)
    h = 2 * z + x
    barrier = pltpu.get_barrier_semaphore()
    for k in range(2 * planes):

        @pl.when(jnp.logical_and(gets, jnp.logical_or(mine != z, h != k)))
        def _():
            pl.semaphore_signal(
                barrier, inc=1, device_id={"gx": z, "gy": k}, device_id_type=MESH
            )

    greet_line(planes, z, x, (other_core, other_y), 4 - jnp.where(mine == z, 1, 0))
    tall = wo.shape[0] // 2
    across = wo.shape[1] // 2

    def cut_copy(ty, tx, head):
        return pltpu.make_async_remote_copy(
            src_ref=halves.at[tx, pl.ds(ty * tall, tall)],
            dst_ref=cols.at[head, pl.ds(ty * tall, tall)],
            send_sem=o_send.at[ty, tx],
            recv_sem=o_recv.at[head],
            device_id={"gx": 2 * ty + core, "gy": 2 * mine + tx},
            device_id_type=MESH,
        )

    def own_cut(ty, tx):
        return pltpu.make_async_copy(
            halves.at[tx, pl.ds(ty * tall, tall)],
            cols.at[h, pl.ds(ty * tall, tall)],
            o_send.at[ty, tx],
        )

    def is_own(ty, tx):
        return jnp.logical_and(mine == z, jnp.logical_and(ty == y, tx == x))

    def spread(slot, part_y, index):
        rows = cols.at[:, pl.ds(pl.multiple_of(part_y * tall, 16), tall)]
        return remote(rows, rows, spread_send.at[slot], spread_recv.at[slot], "gx", index)

    def send_cuts():
        halves[0] = wo[:, :across]
        halves[1] = wo[:, across:]
        for ty in (0, 1):
            for tx in (0, 1):

                @pl.when(is_own(ty, tx))
                def _():
                    own_cut(ty, tx).start()

                @pl.when(jnp.logical_not(is_own(ty, tx)))
                def _():
                    cut_copy(ty, tx, h).start()

    def spread_first():
        for ty in (0, 1):
            for tx in (0, 1):

                @pl.when(is_own(ty, tx))
                def _():
                    own_cut(ty, tx).wait()

        @pl.when(gets)
        def _():
            for k in range(2 * planes):

                @pl.when(jnp.logical_or(mine != z, h != k))
                def _():
                    piece = cols.at[k, pl.ds(pl.multiple_of(y * tall, 16), tall)]
                    remote(
                        piece, piece, o_send.at[0, 0], o_recv.at[k], "gx", other_core
                    ).wait_recv()

            spread(0, y, other_y).start()
            spread(1, y, other_core).start()

    def spread_second():
        @pl.when(gets)
        def _():
            spread(0, 1 - y, other_y).wait_recv()
            spread(2, 1 - y, other_core).start()

    def spread_end():
        @pl.when(gets)
        def _():
            spread(0, y, other_y).wait_send()
            spread(1, y, other_core).wait_send()
            spread(2, 1 - y, other_core).wait_send()

        @pl.when(jnp.logical_not(gets))
        def _():
            spread(1, y, other_core).wait_recv()
            spread(2, 1 - y, other_core).wait_recv()

        for ty in (0, 1):
            for tx in (0, 1):

                @pl.when(jnp.logical_not(is_own(ty, tx)))
                def _():
                    cut_copy(ty, tx, h).wait_send()

    def place(oz, ox, p):
        first, count = ranges[p]
        return rows_buf.at[pl.ds(pl.multiple_of((2 * oz + ox) * shard + first, 16), count)]

    def own(p):
        first, count = ranges[p]
        return x_ref.at[pl.ds(first, count)]

    def to_x(oz, ox, p, src):
        return remote(
            src, place(oz, ox, p), x_send.at[oz, p], recv.at[2 * oz + ox, p], "gy", 2 * z + 1 - x
        )

    def to_up(oz, ox, p, src):
        return remote(
            src,
            place(oz, ox, p),
            up_send.at[2 * oz + ox, p],
            recv.at[2 * oz + ox, p],
            "gy",
            2 * jnp.minimum(z + 1, planes - 1) + x,
        )

    def to_down(oz, ox, p, src):
        return remote(
            src,
            place(oz, ox, p),
            down_send.at[2 * oz + ox, p],
            recv.at[2 * oz + ox, p],
            "gy",
            2 * jnp.maximum(z - 1, 0) + x,
        )

    def arrived(oz, ox, p):
        ref = place(oz, ox, p)
        remote(ref, ref, x_send.at[0, 0], recv.at[2 * oz + ox, p], "gy", 2 * z + 1 - x).wait_recv()

    def both_ways(oz, ox, p, src):
        @pl.when(z < planes - 1)
        def _():
            to_up(oz, ox, p, src).start()

        @pl.when(z > 0)
        def _():
            to_down(oz, ox, p, src).start()

    to_x(z, x, 2, own(2)).start()
    for p in (0, 1, 2):
        both_ways(z, x, p, own(p))
        if p < 2:
            to_x(z, x, p, own(p)).start()
    mine_copy = pltpu.make_async_copy(
        x_ref, rows_buf.at[pl.ds(pl.multiple_of((2 * z + x) * shard, 16), shard)], w_sem.at[4]
    )
    mine_copy.start()
    send_cuts()
    arrived(z, 1 - x, 2)
    both_ways(z, 1 - x, 2, place(z, 1 - x, 2))
    for load in loads:
        load.wait()
    mine_copy.wait()

    def from_side(oz, below, p, ox):
        @pl.when(jnp.logical_and(oz >= 0, oz < planes))
        def _():
            arrived(oz, ox, p)
            src = place(oz, ox, p)
            if below:

                @pl.when(z < planes - 1)
                def _():
                    to_up(oz, ox, p, src).start()
            else:

                @pl.when(z > 0)
                def _():
                    to_down(oz, ox, p, src).start()

    def from_sides(distance, p, ox, cross):
        for below in (True, False):
            oz = z - distance if below else z + distance
            from_side(oz, below, p, ox)
            if cross:

                @pl.when(jnp.logical_and(oz >= 0, oz < planes))
                def _():
                    to_x(oz, x, p, place(oz, x, p)).start()

    def group_at(k):
        last = planes - 1
        low = jnp.where(z == 0, k, jnp.where(k == 0, 1, jnp.where(k == 1, 0, k)))
        m = last - z
        high = jnp.where(m == 0, k, jnp.where(k == 0, 1, jnp.where(k == 1, 0, k)))
        return jnp.where(z < 2, low, last - high)

    def core_copy(g):
        return remote(
            part.at[g], core_in.at[g // 2], c_send.at[g // 2], c_recv.at[g // 2], "gx", other_core
        )

    def y_copy():
        return remote(y_out, y_in, y_send.at[0], y_recv.at[0], "gx", other_y)

    def settle(g):
        @pl.when(g - 2 * (g // 2) == core)
        def _():
            core_copy(g).wait_recv()

            @pl.when(g // 2 != y)
            def _():
                y_out[...] = (part[g] + core_in[g // 2]).astype(y_out.dtype)
                y_copy().start()

    def step(k, carry):
        distance = k + 1
        for p in (0, 1):
            from_sides(distance, p, x, True)
        for ox in (x, 1 - x):
            from_sides(distance, 2, ox, False)

        @pl.when(k > 0)
        def _():
            settle(group_at(k - 1))

        @pl.when(k == planes - 2)
        def _():
            spread_first()

        @pl.when(k == planes - 1)
        def _():
            spread_second()

        g = group_at(k)
        for p in (0, 1):
            arrived(g, 1 - x, p)
        part[g] = lax.dot_general(
            weights[...],
            rows_buf[pl.ds(pl.multiple_of(g * group_rows, 16), group_rows)],
            NT,
            preferred_element_type=jnp.float32,
        )

        @pl.when(g - 2 * (g // 2) != core)
        def _():
            core_copy(g).start()

        return carry

    lax.fori_loop(0, planes, step, 0)
    settle(group_at(planes - 1))
    y_copy().wait_recv()
    total = part[mine] + core_in[mine // 2] + y_in[...].astype(jnp.float32)
    middle = total[3 * width :].astype(jnp.bfloat16)
    extra = jnp.dot(up[...], middle, preferred_element_type=jnp.float32)
    out[pl.ds(0, width)] = (total[:width] + extra).astype(jnp.bfloat16)
    out[pl.ds(width, 2 * width)] = total[width : 3 * width].astype(jnp.bfloat16)

    spread_end()
    y_copy().wait_send()
    for half in range(planes // 2):
        core_copy(2 * half + 1 - core).wait_send()
    for oz in range(planes):
        for p in (0, 1):
            to_x(oz, x, p, place(oz, x, p)).wait_send()
        for ox in (0, 1):
            for p in (0, 1, 2):
                if p == 2:
                    sent = oz >= 0
                else:
                    sent = x == ox

                @pl.when(jnp.logical_and(sent, jnp.logical_and(oz <= z, z < planes - 1)))
                def _():
                    to_up(oz, ox, p, place(oz, ox, p)).wait_send()

                @pl.when(jnp.logical_and(sent, jnp.logical_and(oz >= z, z > 0)))
                def _():
                    to_down(oz, ox, p, place(oz, ox, p)).wait_send()

    to_x(z, x, 2, own(2)).wait_send()


def project(
    inputs, query_weight, key_weight, value_weight, adapter_down, adapter_up, out_weight, planes
):
    shard, columns = inputs.shape
    features = 3 * query_weight.shape[0] + adapter_down.shape[0]
    tokens = 2 * shard
    height, half = out_weight.shape[0], out_weight.shape[1] // 2
    dma = pltpu.SemaphoreType.DMA
    vmem = pl.BlockSpec(memory_space=pltpu.VMEM)
    anywhere = pl.BlockSpec(memory_space=pl.ANY)

    def kernel(*refs):
        project_kernel(planes, *refs)

    return pl.pallas_call(
        kernel,
        out_shape=(
            jax.ShapeDtypeStruct((3 * query_weight.shape[0], tokens), jnp.bfloat16),
            jax.ShapeDtypeStruct((2 * planes, height, half), jnp.bfloat16),
        ),
        in_specs=[anywhere, anywhere, anywhere, anywhere, anywhere, vmem, vmem],
        out_specs=(vmem, anywhere),
        scratch_shapes=[
            pltpu.VMEM((2, height, half), jnp.bfloat16),
            dma((2, 2)),
            dma((2 * planes,)),
            dma((3,)),
            dma((3,)),
            pltpu.VMEM((planes * tokens, columns), jnp.bfloat16),
            pltpu.VMEM((features, columns), jnp.bfloat16),
            pltpu.VMEM((planes, features, tokens), jnp.float32),
            pltpu.VMEM((planes // 2, features, tokens), jnp.float32),
            pltpu.VMEM((features, tokens), jnp.bfloat16),
            pltpu.VMEM((features, tokens), jnp.bfloat16),
            dma((5,)),
            dma((2 * planes, 3)),
            dma((2 * planes, 3)),
            dma((planes, 3)),
            dma((2 * planes, 3)),
            dma((planes // 2,)),
            dma((planes // 2,)),
            dma((1,)),
            dma((1,)),
        ],
        compiler_params=pltpu.CompilerParams(
            collective_id=0, has_side_effects=True, vmem_limit_bytes=60 * 1024 * 1024
        ),
        cost_estimate=pl.CostEstimate(
            flops=2 * planes * tokens * columns * features,
            bytes_accessed=2 * (planes * tokens + features) * columns,
            transcendentals=0,
        ),
    )(inputs, query_weight, key_weight, value_weight, adapter_down, adapter_up, out_weight)


def gather_kernel(planes, att, out, local_sem, up_send, down_send, x_send, recv):
    z, x = line_position()
    tokens = att.shape[0]
    late = tokens // 6 // 16 * 16
    ranges = ((0, tokens - late), (tokens - late, late))
    local = pltpu.make_async_copy(att, out.at[2 * z + x], local_sem.at[0])
    local.start()
    greet_line(planes, z, x, ())

    def place(oz, ox, p):
        first, count = ranges[p]
        return out.at[2 * oz + ox, pl.ds(first, count)]

    def own(p):
        first, count = ranges[p]
        return att.at[pl.ds(first, count)]

    def to_x(oz, ox, p, src):
        return remote(
            src, place(oz, ox, p), x_send.at[oz, p], recv.at[2 * oz + ox, p], "gy", 2 * z + 1 - x
        )

    def to_up(oz, ox, p, src):
        return remote(
            src,
            place(oz, ox, p),
            up_send.at[2 * oz + ox, p],
            recv.at[2 * oz + ox, p],
            "gy",
            2 * jnp.minimum(z + 1, planes - 1) + x,
        )

    def to_down(oz, ox, p, src):
        return remote(
            src,
            place(oz, ox, p),
            down_send.at[2 * oz + ox, p],
            recv.at[2 * oz + ox, p],
            "gy",
            2 * jnp.maximum(z - 1, 0) + x,
        )

    def arrived(oz, ox, p):
        ref = place(oz, ox, p)
        remote(ref, ref, x_send.at[0, 0], recv.at[2 * oz + ox, p], "gy", 2 * z + 1 - x).wait_recv()

    def both_ways(oz, ox, p, src):
        @pl.when(z < planes - 1)
        def _():
            to_up(oz, ox, p, src).start()

        @pl.when(z > 0)
        def _():
            to_down(oz, ox, p, src).start()

    to_x(z, x, 1, own(1)).start()
    for p in (0, 1):
        both_ways(z, x, p, own(p))
    to_x(z, x, 0, own(0)).start()
    arrived(z, 1 - x, 1)
    both_ways(z, 1 - x, 1, place(z, 1 - x, 1))

    def step(k, carry):
        for p, same in ((0, True), (1, True), (1, False)):
            ox = x if same else 1 - x
            for below in (True, False):
                oz = z - (k + 1) if below else z + (k + 1)

                @pl.when(jnp.logical_and(oz >= 0, oz < planes))
                def _():
                    arrived(oz, ox, p)
                    src = place(oz, ox, p)
                    if below:

                        @pl.when(z < planes - 1)
                        def _():
                            to_up(oz, ox, p, src).start()
                    else:

                        @pl.when(z > 0)
                        def _():
                            to_down(oz, ox, p, src).start()

                    if p == 0:
                        to_x(oz, ox, p, src).start()

        return carry

    lax.fori_loop(0, planes - 1, step, 0)
    local.wait()
    for oz in range(planes):
        arrived(oz, 1 - x, 0)
        to_x(oz, x, 0, place(oz, x, 0)).wait_send()
        for ox in (0, 1):
            for p in (0, 1):
                sent = oz >= 0 if p == 1 else x == ox

                @pl.when(jnp.logical_and(sent, jnp.logical_and(oz <= z, z < planes - 1)))
                def _():
                    to_up(oz, ox, p, place(oz, ox, p)).wait_send()

                @pl.when(jnp.logical_and(sent, jnp.logical_and(oz >= z, z > 0)))
                def _():
                    to_down(oz, ox, p, place(oz, ox, p)).wait_send()

    to_x(z, x, 1, own(1)).wait_send()


def gather_heads(att, planes):
    dma = pltpu.SemaphoreType.DMA
    vmem = pl.BlockSpec(memory_space=pltpu.VMEM)

    def kernel(*refs):
        gather_kernel(planes, *refs)

    return pl.pallas_call(
        kernel,
        out_shape=jax.ShapeDtypeStruct((2 * planes,) + att.shape, jnp.bfloat16),
        in_specs=[vmem],
        out_specs=vmem,
        scratch_shapes=[
            dma((1,)),
            dma((2 * planes, 2)),
            dma((2 * planes, 2)),
            dma((planes, 2)),
            dma((2 * planes, 2)),
        ],
        compiler_params=pltpu.CompilerParams(
            collective_id=1, has_side_effects=True, vmem_limit_bytes=16 * 1024 * 1024
        ),
    )(att)


def per_device(
    inputs,
    query_weight,
    key_weight,
    value_weight,
    adapter_down,
    adapter_up,
    prompt_keys,
    prompt_values,
    cache_keys,
    cache_values,
    cache_lengths,
    parents,
    out_weight,
):
    requests = cache_keys.shape[0]
    node_count = parents.shape[1]
    local_rows = requests * node_count
    head_width = query_weight.shape[0]
    head_count = head_width // HEAD
    lines = lax.axis_size("gx") == 4 and lax.axis_size("gy") == 8
    shaped = (requests, node_count, head_count, HEAD)
    cached = (requests, head_count, HEAD, cache_keys.shape[2])
    reached = ancestors(parents)
    if lines:
        planes = lax.axis_size("gy") // 2
        projected, columns = project(
            inputs,
            query_weight,
            key_weight,
            value_weight,
            adapter_down,
            adapter_up,
            out_weight,
            planes,
        )
        queries = projected[:head_width].T
        new_keys = projected[head_width : 2 * head_width].T
        new_values = projected[2 * head_width :].T
    else:
        all_rows = lax.all_gather(inputs, "gy", axis=0, tiled=True)
        mixture = lax.psum_scatter(
            jnp.concatenate(
                [
                    contract_rows(all_rows, matrix)
                    for matrix in (query_weight, key_weight, value_weight, adapter_down)
                ],
                axis=1,
            ),
            "gx",
            scatter_dimension=0,
            tiled=True,
        )
        query_base = mixture[:, :head_width]
        new_keys = mixture[:, head_width : 2 * head_width].astype(jnp.bfloat16)
        new_values = mixture[:, 2 * head_width : 3 * head_width].astype(jnp.bfloat16)
        adapter_mid = mixture[:, 3 * head_width :].astype(jnp.bfloat16)
        queries = (query_base + contract_rows(adapter_mid, adapter_up)).astype(jnp.bfloat16)
    attended = attend(
        queries.reshape(shaped),
        new_keys.reshape(shaped),
        new_values.reshape(shaped),
        prompt_keys,
        prompt_values,
        cache_keys.reshape(cached),
        cache_values.reshape(cached),
        cache_lengths,
        reached,
    )
    flattened = attended.reshape(local_rows, head_width)
    if lines:
        everyone = gather_heads(flattened, planes)
        return jnp.einsum(
            "hre,hec->rc", everyone, columns, preferred_element_type=jnp.float32
        ).astype(jnp.bfloat16)
    partial_sums = jnp.dot(
        flattened,
        lax.all_gather(out_weight, "gx", axis=1, tiled=True),
        preferred_element_type=jnp.float32,
    )
    return lax.psum_scatter(
        partial_sums.astype(jnp.bfloat16), "gy", scatter_dimension=1, tiled=True
    )


def solution(mesh):
    placed = (
        P("gy", "gx"),
        P("gy", "gx"),
        P("gy", "gx"),
        P("gy", "gx"),
        P(None, "gx"),
        P("gy", None),
        P("gx", "gy", None),
        P("gx", "gy", None),
        P("gx", "gy", None),
        P("gx", "gy", None),
        P("gx"),
        P("gx", None),
        P("gy", "gx"),
    )
    return jax.shard_map(
        per_device, mesh=mesh, in_specs=placed, out_specs=P("gx", "gy"), check_vma=False
    )
```

```python
import math

import jax
import jax.numpy as jnp
from jax import lax
from jax.experimental import pallas as pl
from jax.experimental.pallas import tpu as pltpu
from jax.sharding import PartitionSpec as P

HEAD = 224
NT = (((1,), (1,)), ((), ()))
MESH = pl.DeviceIdType.MESH


def contract_rows(left, right):
    return lax.dot_general(left, right, NT, preferred_element_type=jnp.float32)


def ancestors(parents):
    node_count = parents.shape[1]
    columns = jnp.arange(node_count, dtype=jnp.int32)
    parent_hot = (parents[:, :, None] == columns[None, None, :]).astype(jnp.float32)
    reached = jnp.minimum(jnp.eye(node_count, dtype=jnp.float32)[None] + parent_hot, 1.0)
    reached = reached.astype(jnp.bfloat16)
    rounds = max(1, math.ceil(math.log2(node_count)))
    for sweep in range(rounds):
        step = jnp.einsum("rnm,rmk->rnk", reached, reached, preferred_element_type=jnp.float32)
        reached = jnp.minimum(reached.astype(jnp.float32) + step, 1.0).astype(jnp.bfloat16)
    return reached


def attend(queries, new_keys, new_values, prompt_k, prompt_v, cache_k, cache_v, lengths, reached):
    factor = 1.0 / math.sqrt(queries.shape[-1])
    s_prompt = (
        jnp.einsum("rnhe,hep->rnhp", queries, prompt_k, preferred_element_type=jnp.float32) * factor
    )
    s_cache = (
        jnp.einsum("rnhe,rhec->rnhc", queries, cache_k, preferred_element_type=jnp.float32) * factor
    )
    s_tree = (
        jnp.einsum("rnhe,rmhe->rnhm", queries, new_keys, preferred_element_type=jnp.float32)
        * factor
    )
    usable = jnp.arange(cache_k.shape[-1], dtype=jnp.int32)[None, :] < lengths[:, None]
    s_cache = jnp.where(usable[:, None, None, :], s_cache, -jnp.inf)
    s_tree = jnp.where(reached[:, :, None, :] > 0.5, s_tree, -jnp.inf)
    largest = jnp.maximum(
        jnp.maximum(
            jnp.max(s_prompt, axis=-1, keepdims=True), jnp.max(s_cache, axis=-1, keepdims=True)
        ),
        jnp.max(s_tree, axis=-1, keepdims=True),
    )
    e_prompt = jnp.exp(s_prompt - largest)
    e_cache = jnp.exp(s_cache - largest)
    e_tree = jnp.exp(s_tree - largest)
    totals = (
        jnp.sum(e_prompt, axis=-1, keepdims=True)
        + jnp.sum(e_cache, axis=-1, keepdims=True)
        + jnp.sum(e_tree, axis=-1, keepdims=True)
    )
    w_prompt = (e_prompt / totals).astype(jnp.bfloat16)
    w_cache = (e_cache / totals).astype(jnp.bfloat16)
    w_tree = (e_tree / totals).astype(jnp.bfloat16)
    result = jnp.einsum("rnhp,hep->rnhe", w_prompt, prompt_v, preferred_element_type=jnp.float32)
    result = result + jnp.einsum(
        "rnhc,rhec->rnhe", w_cache, cache_v, preferred_element_type=jnp.float32
    )
    result = result + jnp.einsum(
        "rnhm,rmhe->rnhe", w_tree, new_values, preferred_element_type=jnp.float32
    )
    return result.astype(jnp.bfloat16)


def remote(src, dst, send, recv, axis, index):
    return pltpu.make_async_remote_copy(
        src_ref=src,
        dst_ref=dst,
        send_sem=send,
        recv_sem=recv,
        device_id={axis: index},
        device_id_type=MESH,
    )


def line_position():
    h = lax.axis_index("gy")
    z = h // 2
    x = h - 2 * z
    return z, x


def greet_line(planes, z, x, extra):
    barrier = pltpu.get_barrier_semaphore()

    def signal(axis, index):
        pl.semaphore_signal(barrier, inc=1, device_id={axis: index}, device_id_type=MESH)

    signal("gy", 2 * z + 1 - x)
    for index in extra:
        signal("gx", index)

    @pl.when(z > 0)
    def _():
        signal("gy", 2 * (z - 1) + x)

    @pl.when(z < planes - 1)
    def _():
        signal("gy", 2 * (z + 1) + x)

    inner = jnp.where(z > 0, 1, 0) + jnp.where(z < planes - 1, 1, 0)
    pl.semaphore_wait(barrier, 1 + len(extra) + inner)


def pieces_of(rows):
    late = rows // 6
    half = (rows - late) // 2
    return ((0, half), (half, half), (2 * half, late))


def project_kernel(
    planes,
    x_ref,
    wq,
    wk,
    wv,
    wd,
    up,
    wo,
    out,
    cols,
    spread_send,
    spread_recv,
    rows_buf,
    weights,
    part,
    core_in,
    y_out,
    y_in,
    w_sem,
    up_send,
    down_send,
    x_send,
    recv,
    c_send,
    c_recv,
    y_send,
    y_recv,
):
    z, x = line_position()
    mine = lax.axis_index("gx")
    y = mine // 2
    core = mine - 2 * y
    other_core = 2 * y + 1 - core
    other_y = 2 * (1 - y) + core
    shard = x_ref.shape[0]
    group_rows = 2 * shard
    ranges = pieces_of(shard)
    width = wq.shape[0]

    loads = []
    start = 0
    for slot, matrix in enumerate((wq, wk, wv, wd)):
        count = matrix.shape[0]
        load = pltpu.make_async_copy(
            matrix, weights.at[pl.ds(start, count)], w_sem.at[slot]
        )
        load.start()
        loads.append(load)
        start += count

    greet_line(planes, z, x, (other_core, other_y))

    own_block = pltpu.make_async_copy(wo, cols.at[mine], w_sem.at[5])

    def block_copy(slot, index, target, src):
        return remote(
            src, cols.at[index], spread_send.at[slot], spread_recv.at[slot], "gx", target
        )

    def spread_start():
        own_block.start()
        block_copy(0, mine, other_y, wo).start()
        block_copy(1, mine, other_core, wo).start()

    def spread_second():
        block_copy(0, other_y, other_y, cols.at[other_y]).wait_recv()
        block_copy(2, other_y, other_core, cols.at[other_y]).start()

    def spread_end():
        own_block.wait()
        block_copy(0, mine, other_y, wo).wait_send()
        block_copy(1, mine, other_core, wo).wait_send()
        block_copy(2, other_y, other_core, cols.at[other_y]).wait_send()
        block_copy(1, other_core, other_core, cols.at[other_core]).wait_recv()
        cross = 2 * (1 - y) + 1 - core
        block_copy(2, cross, other_core, cols.at[cross]).wait_recv()

    def place(oz, ox, p):
        first, count = ranges[p]
        return rows_buf.at[pl.ds(pl.multiple_of((2 * oz + ox) * shard + first, 16), count)]

    def own(p):
        first, count = ranges[p]
        return x_ref.at[pl.ds(first, count)]

    def to_x(oz, ox, p, src):
        return remote(
            src, place(oz, ox, p), x_send.at[oz, p], recv.at[2 * oz + ox, p], "gy", 2 * z + 1 - x
        )

    def to_up(oz, ox, p, src):
        return remote(
            src,
            place(oz, ox, p),
            up_send.at[2 * oz + ox, p],
            recv.at[2 * oz + ox, p],
            "gy",
            2 * jnp.minimum(z + 1, planes - 1) + x,
        )

    def to_down(oz, ox, p, src):
        return remote(
            src,
            place(oz, ox, p),
            down_send.at[2 * oz + ox, p],
            recv.at[2 * oz + ox, p],
            "gy",
            2 * jnp.maximum(z - 1, 0) + x,
        )

    def arrived(oz, ox, p):
        ref = place(oz, ox, p)
        remote(ref, ref, x_send.at[0, 0], recv.at[2 * oz + ox, p], "gy", 2 * z + 1 - x).wait_recv()

    def both_ways(oz, ox, p, src):
        @pl.when(z < planes - 1)
        def _():
            to_up(oz, ox, p, src).start()

        @pl.when(z > 0)
        def _():
            to_down(oz, ox, p, src).start()

    to_x(z, x, 2, own(2)).start()
    for p in (0, 1, 2):
        both_ways(z, x, p, own(p))
        if p < 2:
            to_x(z, x, p, own(p)).start()
    mine_copy = pltpu.make_async_copy(
        x_ref, rows_buf.at[pl.ds(pl.multiple_of((2 * z + x) * shard, 16), shard)], w_sem.at[4]
    )
    mine_copy.start()
    spread_start()
    arrived(z, 1 - x, 2)
    both_ways(z, 1 - x, 2, place(z, 1 - x, 2))
    for load in loads:
        load.wait()
    mine_copy.wait()

    def from_side(oz, below, p, ox):
        @pl.when(jnp.logical_and(oz >= 0, oz < planes))
        def _():
            arrived(oz, ox, p)
            src = place(oz, ox, p)
            if below:

                @pl.when(z < planes - 1)
                def _():
                    to_up(oz, ox, p, src).start()
            else:

                @pl.when(z > 0)
                def _():
                    to_down(oz, ox, p, src).start()

    def from_sides(distance, p, ox, cross):
        for below in (True, False):
            oz = z - distance if below else z + distance
            from_side(oz, below, p, ox)
            if cross:

                @pl.when(jnp.logical_and(oz >= 0, oz < planes))
                def _():
                    to_x(oz, x, p, place(oz, x, p)).start()

    def group_at(k):
        last = planes - 1
        low = jnp.where(z == 0, k, jnp.where(k == 0, 1, jnp.where(k == 1, 0, k)))
        m = last - z
        high = jnp.where(m == 0, k, jnp.where(k == 0, 1, jnp.where(k == 1, 0, k)))
        return jnp.where(z < 2, low, last - high)

    def core_copy(g):
        return remote(
            part.at[g], core_in.at[g // 2], c_send.at[g // 2], c_recv.at[g // 2], "gx", other_core
        )

    def y_copy():
        return remote(y_out, y_in, y_send.at[0], y_recv.at[0], "gx", other_y)

    def settle(g):
        @pl.when(g - 2 * (g // 2) == core)
        def _():
            core_copy(g).wait_recv()

            @pl.when(g // 2 != y)
            def _():
                y_out[...] = (part[g] + core_in[g // 2]).astype(y_out.dtype)
                y_copy().start()

    def step(k, carry):
        distance = k + 1
        for p in (0, 1):
            from_sides(distance, p, x, True)
        for ox in (x, 1 - x):
            from_sides(distance, 2, ox, False)

        @pl.when(k > 0)
        def _():
            settle(group_at(k - 1))

        @pl.when(k == 1)
        def _():
            spread_second()

        g = group_at(k)
        for p in (0, 1):
            arrived(g, 1 - x, p)
        part[g] = lax.dot_general(
            weights[...],
            rows_buf[pl.ds(pl.multiple_of(g * group_rows, 16), group_rows)],
            NT,
            preferred_element_type=jnp.float32,
        )

        @pl.when(g - 2 * (g // 2) != core)
        def _():
            core_copy(g).start()

        return carry

    lax.fori_loop(0, planes, step, 0)
    settle(group_at(planes - 1))
    y_copy().wait_recv()
    total = part[mine] + core_in[mine // 2] + y_in[...].astype(jnp.float32)
    middle = total[3 * width :].astype(jnp.bfloat16)
    extra = jnp.dot(up[...], middle, preferred_element_type=jnp.float32)
    out[pl.ds(0, width)] = (total[:width] + extra).astype(jnp.bfloat16)
    out[pl.ds(width, 2 * width)] = total[width : 3 * width].astype(jnp.bfloat16)

    spread_end()
    y_copy().wait_send()
    for half in range(planes // 2):
        core_copy(2 * half + 1 - core).wait_send()
    for oz in range(planes):
        for p in (0, 1):
            to_x(oz, x, p, place(oz, x, p)).wait_send()
        for ox in (0, 1):
            for p in (0, 1, 2):
                if p == 2:
                    sent = oz >= 0
                else:
                    sent = x == ox

                @pl.when(jnp.logical_and(sent, jnp.logical_and(oz <= z, z < planes - 1)))
                def _():
                    to_up(oz, ox, p, place(oz, ox, p)).wait_send()

                @pl.when(jnp.logical_and(sent, jnp.logical_and(oz >= z, z > 0)))
                def _():
                    to_down(oz, ox, p, place(oz, ox, p)).wait_send()

    to_x(z, x, 2, own(2)).wait_send()


def project(
    inputs, query_weight, key_weight, value_weight, adapter_down, adapter_up, out_weight, planes
):
    shard, columns = inputs.shape
    features = 3 * query_weight.shape[0] + adapter_down.shape[0]
    tokens = 2 * shard
    dma = pltpu.SemaphoreType.DMA
    vmem = pl.BlockSpec(memory_space=pltpu.VMEM)
    anywhere = pl.BlockSpec(memory_space=pl.ANY)

    def kernel(*refs):
        project_kernel(planes, *refs)

    return pl.pallas_call(
        kernel,
        out_shape=(
            jax.ShapeDtypeStruct((3 * query_weight.shape[0], tokens), jnp.bfloat16),
            jax.ShapeDtypeStruct((planes,) + out_weight.shape, jnp.bfloat16),
        ),
        in_specs=[anywhere, anywhere, anywhere, anywhere, anywhere, vmem, anywhere],
        out_specs=(vmem, anywhere),
        scratch_shapes=[
            dma((3,)),
            dma((3,)),
            pltpu.VMEM((planes * tokens, columns), jnp.bfloat16),
            pltpu.VMEM((features, columns), jnp.bfloat16),
            pltpu.VMEM((planes, features, tokens), jnp.float32),
            pltpu.VMEM((planes // 2, features, tokens), jnp.float32),
            pltpu.VMEM((features, tokens), jnp.bfloat16),
            pltpu.VMEM((features, tokens), jnp.bfloat16),
            dma((6,)),
            dma((2 * planes, 3)),
            dma((2 * planes, 3)),
            dma((planes, 3)),
            dma((2 * planes, 3)),
            dma((planes // 2,)),
            dma((planes // 2,)),
            dma((1,)),
            dma((1,)),
        ],
        compiler_params=pltpu.CompilerParams(
            collective_id=0, has_side_effects=True, vmem_limit_bytes=60 * 1024 * 1024
        ),
        cost_estimate=pl.CostEstimate(
            flops=2 * planes * tokens * columns * features,
            bytes_accessed=2 * (planes * tokens + features) * columns,
            transcendentals=0,
        ),
    )(inputs, query_weight, key_weight, value_weight, adapter_down, adapter_up, out_weight)


def output_kernel(
    planes,
    att,
    weight,
    out,
    x_out,
    x_in,
    kept,
    z_out,
    up_in,
    down_in,
    x_send,
    x_recv,
    z_send,
    up_recv,
    down_recv,
):
    z, x = line_position()
    block = out.shape[0]
    greet_line(planes, z, x, ())

    def plane_at(k):
        last = planes - 1
        low = jnp.where(z == 0, last - k, jnp.where(k == 0, 3, jnp.where(k == 1, 0, 3 - k + 1)))
        low = jnp.where(jnp.logical_and(z == 1, k == 3), 1, low)
        m = last - z
        high = jnp.where(m == 0, last - k, jnp.where(k == 0, 3, jnp.where(k == 1, 0, 3 - k + 1)))
        high = jnp.where(jnp.logical_and(m == 1, k == 3), 1, high)
        return jnp.where(z < 2, low, last - high)

    def x_copy(oz):
        return remote(
            x_out.at[oz], x_in.at[oz], x_send.at[oz], x_recv.at[oz], "gy", 2 * z + 1 - x
        )

    def up_copy(oz):
        return remote(
            z_out.at[oz],
            up_in.at[oz],
            z_send.at[oz],
            up_recv.at[oz],
            "gy",
            2 * jnp.minimum(z + 1, planes - 1) + x,
        )

    def down_copy(oz):
        return remote(
            z_out.at[oz],
            down_in.at[oz],
            z_send.at[oz],
            down_recv.at[oz],
            "gy",
            2 * jnp.maximum(z - 1, 0) + x,
        )

    def cross(k, carry):
        oz = plane_at(k)
        both = lax.dot_general(
            weight[oz], att[...], (((0,), (0,)), ((), ())), preferred_element_type=jnp.float32
        )
        low, high = both[:block], both[block:]
        x_out[oz] = jnp.where(x == 0, high, low).astype(x_out.dtype)
        x_copy(oz).start()
        kept[oz] = jnp.where(x == 0, low, high)
        return carry

    lax.fori_loop(0, planes, cross, 0)

    def along(k, carry):
        oz = plane_at(k)
        x_copy(oz).wait_recv()
        kept[oz] = kept[oz] + x_in[oz].astype(jnp.float32)

        @pl.when(jnp.logical_and(z > 0, oz >= z))
        def _():
            up_copy(oz).wait_recv()
            kept[oz] = kept[oz] + up_in[oz].astype(jnp.float32)

        @pl.when(jnp.logical_and(z < planes - 1, oz <= z))
        def _():
            down_copy(oz).wait_recv()
            kept[oz] = kept[oz] + down_in[oz].astype(jnp.float32)

        @pl.when(oz > z)
        def _():
            z_out[oz] = kept[oz].astype(z_out.dtype)
            up_copy(oz).start()

        @pl.when(oz < z)
        def _():
            z_out[oz] = kept[oz].astype(z_out.dtype)
            down_copy(oz).start()

        return carry

    lax.fori_loop(0, planes, along, 0)
    out[...] = kept[z].astype(out.dtype)

    def finish(oz, carry):
        x_copy(oz).wait_send()

        @pl.when(oz != z)
        def _():
            up_copy(oz).wait_send()

        return carry

    lax.fori_loop(0, planes, finish, 0)


def project_out(att, weight, planes):
    tokens = att.shape[1]
    block = weight.shape[2] // 2
    dma = pltpu.SemaphoreType.DMA
    vmem = pl.BlockSpec(memory_space=pltpu.VMEM)
    blocks = (planes, block, tokens)

    def kernel(*refs):
        output_kernel(planes, *refs)

    return pl.pallas_call(
        kernel,
        out_shape=jax.ShapeDtypeStruct((block, tokens), jnp.bfloat16),
        in_specs=[vmem, vmem],
        out_specs=vmem,
        scratch_shapes=[
            pltpu.VMEM(blocks, jnp.bfloat16),
            pltpu.VMEM(blocks, jnp.bfloat16),
            pltpu.VMEM(blocks, jnp.float32),
            pltpu.VMEM(blocks, jnp.bfloat16),
            pltpu.VMEM(blocks, jnp.bfloat16),
            pltpu.VMEM(blocks, jnp.bfloat16),
            dma((planes,)),
            dma((planes,)),
            dma((planes,)),
            dma((planes,)),
            dma((planes,)),
        ],
        compiler_params=pltpu.CompilerParams(
            collective_id=1, has_side_effects=True, vmem_limit_bytes=32 * 1024 * 1024
        ),
    )(att, weight)


def per_device(
    inputs,
    query_weight,
    key_weight,
    value_weight,
    adapter_down,
    adapter_up,
    prompt_keys,
    prompt_values,
    cache_keys,
    cache_values,
    cache_lengths,
    parents,
    out_weight,
):
    requests = cache_keys.shape[0]
    node_count = parents.shape[1]
    local_rows = requests * node_count
    head_width = query_weight.shape[0]
    head_count = head_width // HEAD
    lines = lax.axis_size("gx") == 4 and lax.axis_size("gy") == 8
    shaped = (requests, node_count, head_count, HEAD)
    cached = (requests, head_count, HEAD, cache_keys.shape[2])
    reached = ancestors(parents)
    if lines:
        planes = lax.axis_size("gy") // 2
        projected, columns = project(
            inputs,
            query_weight,
            key_weight,
            value_weight,
            adapter_down,
            adapter_up,
            out_weight,
            planes,
        )
        queries = projected[:head_width].T
        new_keys = projected[head_width : 2 * head_width].T
        new_values = projected[2 * head_width :].T
    else:
        all_rows = lax.all_gather(inputs, "gy", axis=0, tiled=True)
        mixture = lax.psum_scatter(
            jnp.concatenate(
                [
                    contract_rows(all_rows, matrix)
                    for matrix in (query_weight, key_weight, value_weight, adapter_down)
                ],
                axis=1,
            ),
            "gx",
            scatter_dimension=0,
            tiled=True,
        )
        query_base = mixture[:, :head_width]
        new_keys = mixture[:, head_width : 2 * head_width].astype(jnp.bfloat16)
        new_values = mixture[:, 2 * head_width : 3 * head_width].astype(jnp.bfloat16)
        adapter_mid = mixture[:, 3 * head_width :].astype(jnp.bfloat16)
        queries = (query_base + contract_rows(adapter_mid, adapter_up)).astype(jnp.bfloat16)
    attended = attend(
        queries.reshape(shaped),
        new_keys.reshape(shaped),
        new_values.reshape(shaped),
        prompt_keys,
        prompt_values,
        cache_keys.reshape(cached),
        cache_values.reshape(cached),
        cache_lengths,
        reached,
    )
    flattened = attended.reshape(local_rows, head_width)
    if lines:
        return project_out(flattened.T, columns, planes).T
    partial_sums = jnp.dot(
        flattened,
        lax.all_gather(out_weight, "gx", axis=1, tiled=True),
        preferred_element_type=jnp.float32,
    )
    return lax.psum_scatter(
        partial_sums.astype(jnp.bfloat16), "gy", scatter_dimension=1, tiled=True
    )


def solution(mesh):
    placed = (
        P("gy", "gx"),
        P("gy", "gx"),
        P("gy", "gx"),
        P("gy", "gx"),
        P(None, "gx"),
        P("gy", None),
        P("gx", "gy", None),
        P("gx", "gy", None),
        P("gx", "gy", None),
        P("gx", "gy", None),
        P("gx"),
        P("gx", None),
        P("gy", "gx"),
    )
    return jax.shard_map(
        per_device, mesh=mesh, in_specs=placed, out_specs=P("gx", "gy"), check_vma=False
    )
```

```python
import math

import jax
import jax.numpy as jnp
from jax import lax
from jax.experimental import pallas as pl
from jax.experimental.pallas import tpu as pltpu
from jax.sharding import PartitionSpec as P

HEAD = 224
NT = (((1,), (1,)), ((), ()))
MESH = pl.DeviceIdType.MESH


def contract_rows(left, right):
    return lax.dot_general(left, right, NT, preferred_element_type=jnp.float32)


def ancestors(parents):
    node_count = parents.shape[1]
    columns = jnp.arange(node_count, dtype=jnp.int32)
    parent_hot = (parents[:, :, None] == columns[None, None, :]).astype(jnp.float32)
    reached = jnp.minimum(jnp.eye(node_count, dtype=jnp.float32)[None] + parent_hot, 1.0)
    reached = reached.astype(jnp.bfloat16)
    rounds = max(1, math.ceil(math.log2(node_count)))
    for sweep in range(rounds):
        step = jnp.einsum("rnm,rmk->rnk", reached, reached, preferred_element_type=jnp.float32)
        reached = jnp.minimum(reached.astype(jnp.float32) + step, 1.0).astype(jnp.bfloat16)
    return reached


def attend(queries, new_keys, new_values, prompt_k, prompt_v, cache_k, cache_v, lengths, reached):
    factor = 1.0 / math.sqrt(queries.shape[-1])
    s_prompt = (
        jnp.einsum("rnhe,hep->rnhp", queries, prompt_k, preferred_element_type=jnp.float32) * factor
    )
    s_cache = (
        jnp.einsum("rnhe,rhec->rnhc", queries, cache_k, preferred_element_type=jnp.float32) * factor
    )
    s_tree = (
        jnp.einsum("rnhe,rmhe->rnhm", queries, new_keys, preferred_element_type=jnp.float32)
        * factor
    )
    usable = jnp.arange(cache_k.shape[-1], dtype=jnp.int32)[None, :] < lengths[:, None]
    s_cache = jnp.where(usable[:, None, None, :], s_cache, -jnp.inf)
    s_tree = jnp.where(reached[:, :, None, :] > 0.5, s_tree, -jnp.inf)
    largest = jnp.maximum(
        jnp.maximum(
            jnp.max(s_prompt, axis=-1, keepdims=True), jnp.max(s_cache, axis=-1, keepdims=True)
        ),
        jnp.max(s_tree, axis=-1, keepdims=True),
    )
    e_prompt = jnp.exp(s_prompt - largest)
    e_cache = jnp.exp(s_cache - largest)
    e_tree = jnp.exp(s_tree - largest)
    totals = (
        jnp.sum(e_prompt, axis=-1, keepdims=True)
        + jnp.sum(e_cache, axis=-1, keepdims=True)
        + jnp.sum(e_tree, axis=-1, keepdims=True)
    )
    w_prompt = (e_prompt / totals).astype(jnp.bfloat16)
    w_cache = (e_cache / totals).astype(jnp.bfloat16)
    w_tree = (e_tree / totals).astype(jnp.bfloat16)
    result = jnp.einsum("rnhp,hep->rnhe", w_prompt, prompt_v, preferred_element_type=jnp.float32)
    result = result + jnp.einsum(
        "rnhc,rhec->rnhe", w_cache, cache_v, preferred_element_type=jnp.float32
    )
    result = result + jnp.einsum(
        "rnhm,rmhe->rnhe", w_tree, new_values, preferred_element_type=jnp.float32
    )
    return result.astype(jnp.bfloat16)


def remote(src, dst, send, recv, axis, index):
    return pltpu.make_async_remote_copy(
        src_ref=src,
        dst_ref=dst,
        send_sem=send,
        recv_sem=recv,
        device_id={axis: index},
        device_id_type=MESH,
    )


def line_position():
    h = lax.axis_index("gy")
    z = h // 2
    x = h - 2 * z
    return z, x


def greet_line(planes, z, x, extra):
    barrier = pltpu.get_barrier_semaphore()

    def signal(axis, index):
        pl.semaphore_signal(barrier, inc=1, device_id={axis: index}, device_id_type=MESH)

    signal("gy", 2 * z + 1 - x)
    for index in extra:
        signal("gx", index)

    @pl.when(z > 0)
    def _():
        signal("gy", 2 * (z - 1) + x)

    @pl.when(z < planes - 1)
    def _():
        signal("gy", 2 * (z + 1) + x)

    inner = jnp.where(z > 0, 1, 0) + jnp.where(z < planes - 1, 1, 0)
    pl.semaphore_wait(barrier, 1 + len(extra) + inner)


def pieces_of(rows):
    late = rows // 6
    half = (rows - late) // 2
    return ((0, half), (half, half), (2 * half, late))


def project_kernel(
    planes,
    x_ref,
    wq,
    wk,
    wv,
    wd,
    up,
    wo,
    out,
    cols,
    spread_send,
    spread_recv,
    rows_buf,
    weights,
    part,
    core_in,
    y_out,
    y_in,
    w_sem,
    up_send,
    down_send,
    x_send,
    recv,
    c_send,
    c_recv,
    y_send,
    y_recv,
):
    z, x = line_position()
    mine = lax.axis_index("gx")
    y = mine // 2
    core = mine - 2 * y
    other_core = 2 * y + 1 - core
    other_y = 2 * (1 - y) + core
    shard = x_ref.shape[0]
    group_rows = 2 * shard
    ranges = pieces_of(shard)
    width = wq.shape[0]

    loads = []
    start = 0
    for slot, matrix in enumerate((wq, wk, wv, wd)):
        count = matrix.shape[0]
        load = pltpu.make_async_copy(
            matrix, weights.at[pl.ds(start, count)], w_sem.at[slot]
        )
        load.start()
        loads.append(load)
        start += count

    greet_line(planes, z, x, (other_core, other_y))

    own_block = pltpu.make_async_copy(wo, cols.at[mine], w_sem.at[5])

    def block_copy(slot, index, target, src):
        return remote(
            src, cols.at[index], spread_send.at[slot], spread_recv.at[slot], "gx", target
        )

    def spread_start():
        own_block.start()
        block_copy(0, mine, other_y, wo).start()
        block_copy(1, mine, other_core, wo).start()

    def spread_second():
        block_copy(0, other_y, other_y, cols.at[other_y]).wait_recv()
        block_copy(2, other_y, other_core, cols.at[other_y]).start()

    def spread_end():
        own_block.wait()
        block_copy(0, mine, other_y, wo).wait_send()
        block_copy(1, mine, other_core, wo).wait_send()
        block_copy(2, other_y, other_core, cols.at[other_y]).wait_send()
        block_copy(1, other_core, other_core, cols.at[other_core]).wait_recv()
        cross = 2 * (1 - y) + 1 - core
        block_copy(2, cross, other_core, cols.at[cross]).wait_recv()

    def place(oz, ox, p):
        first, count = ranges[p]
        return rows_buf.at[pl.ds(pl.multiple_of((2 * oz + ox) * shard + first, 16), count)]

    def own(p):
        first, count = ranges[p]
        return x_ref.at[pl.ds(first, count)]

    def to_x(oz, ox, p, src):
        return remote(
            src, place(oz, ox, p), x_send.at[oz, p], recv.at[2 * oz + ox, p], "gy", 2 * z + 1 - x
        )

    def to_up(oz, ox, p, src):
        return remote(
            src,
            place(oz, ox, p),
            up_send.at[2 * oz + ox, p],
            recv.at[2 * oz + ox, p],
            "gy",
            2 * jnp.minimum(z + 1, planes - 1) + x,
        )

    def to_down(oz, ox, p, src):
        return remote(
            src,
            place(oz, ox, p),
            down_send.at[2 * oz + ox, p],
            recv.at[2 * oz + ox, p],
            "gy",
            2 * jnp.maximum(z - 1, 0) + x,
        )

    def arrived(oz, ox, p):
        ref = place(oz, ox, p)
        remote(ref, ref, x_send.at[0, 0], recv.at[2 * oz + ox, p], "gy", 2 * z + 1 - x).wait_recv()

    def both_ways(oz, ox, p, src):
        @pl.when(z < planes - 1)
        def _():
            to_up(oz, ox, p, src).start()

        @pl.when(z > 0)
        def _():
            to_down(oz, ox, p, src).start()

    to_x(z, x, 2, own(2)).start()
    for p in (0, 1, 2):
        both_ways(z, x, p, own(p))
        if p < 2:
            to_x(z, x, p, own(p)).start()
    mine_copy = pltpu.make_async_copy(
        x_ref, rows_buf.at[pl.ds(pl.multiple_of((2 * z + x) * shard, 16), shard)], w_sem.at[4]
    )
    mine_copy.start()
    spread_start()
    arrived(z, 1 - x, 2)
    both_ways(z, 1 - x, 2, place(z, 1 - x, 2))
    for load in loads:
        load.wait()
    mine_copy.wait()

    def from_side(oz, below, p, ox):
        @pl.when(jnp.logical_and(oz >= 0, oz < planes))
        def _():
            arrived(oz, ox, p)
            src = place(oz, ox, p)
            if below:

                @pl.when(z < planes - 1)
                def _():
                    to_up(oz, ox, p, src).start()
            else:

                @pl.when(z > 0)
                def _():
                    to_down(oz, ox, p, src).start()

    def from_sides(distance, p, ox, cross):
        for below in (True, False):
            oz = z - distance if below else z + distance
            from_side(oz, below, p, ox)
            if cross:

                @pl.when(jnp.logical_and(oz >= 0, oz < planes))
                def _():
                    to_x(oz, x, p, place(oz, x, p)).start()

    def group_at(k):
        last = planes - 1
        low = jnp.where(z == 0, k, jnp.where(k == 0, 1, jnp.where(k == 1, 0, k)))
        m = last - z
        high = jnp.where(m == 0, k, jnp.where(k == 0, 1, jnp.where(k == 1, 0, k)))
        return jnp.where(z < 2, low, last - high)

    span = weights.shape[0] // 2

    def core_copy(g, i):
        lines = pl.ds(i * span, span)
        return remote(
            part.at[g, lines],
            core_in.at[g // 2, lines],
            c_send.at[g // 2, i],
            c_recv.at[g // 2, i],
            "gx",
            other_core,
        )

    def y_copy(i):
        lines = pl.ds(i * span, span)
        return remote(y_out.at[lines], y_in.at[lines], y_send.at[i], y_recv.at[i], "gx", other_y)

    def settle(g):
        @pl.when(g - 2 * (g // 2) == core)
        def _():
            for i in (0, 1):
                lines = pl.ds(i * span, span)
                core_copy(g, i).wait_recv()

                @pl.when(g // 2 != y)
                def _():
                    y_out[lines] = (part[g, lines] + core_in[g // 2, lines]).astype(y_out.dtype)
                    y_copy(i).start()

    def step(k, carry):
        distance = k + 1
        for p in (0, 1):
            from_sides(distance, p, x, True)
        for ox in (x, 1 - x):
            from_sides(distance, 2, ox, False)

        @pl.when(k > 0)
        def _():
            settle(group_at(k - 1))

        @pl.when(k == 1)
        def _():
            spread_second()

        g = group_at(k)
        for p in (0, 1):
            arrived(g, 1 - x, p)
        for i in (0, 1):
            lines = pl.ds(i * span, span)
            part[g, lines] = lax.dot_general(
                weights[lines],
                rows_buf[pl.ds(pl.multiple_of(g * group_rows, 16), group_rows)],
                NT,
                preferred_element_type=jnp.float32,
            )

            @pl.when(g - 2 * (g // 2) != core)
            def _():
                core_copy(g, i).start()

        return carry

    lax.fori_loop(0, planes, step, 0)
    settle(group_at(planes - 1))
    y_copy(0).wait_recv()
    y_copy(1).wait_recv()
    total = part[mine] + core_in[mine // 2] + y_in[...].astype(jnp.float32)
    middle = total[3 * width :].astype(jnp.bfloat16)
    extra = jnp.dot(up[...], middle, preferred_element_type=jnp.float32)
    out[pl.ds(0, width)] = (total[:width] + extra).astype(jnp.bfloat16)
    out[pl.ds(width, 2 * width)] = total[width : 3 * width].astype(jnp.bfloat16)

    spread_end()
    y_copy(0).wait_send()
    y_copy(1).wait_send()
    for half in range(planes // 2):
        core_copy(2 * half + 1 - core, 0).wait_send()
        core_copy(2 * half + 1 - core, 1).wait_send()
    for oz in range(planes):
        for p in (0, 1):
            to_x(oz, x, p, place(oz, x, p)).wait_send()
        for ox in (0, 1):
            for p in (0, 1, 2):
                if p == 2:
                    sent = oz >= 0
                else:
                    sent = x == ox

                @pl.when(jnp.logical_and(sent, jnp.logical_and(oz <= z, z < planes - 1)))
                def _():
                    to_up(oz, ox, p, place(oz, ox, p)).wait_send()

                @pl.when(jnp.logical_and(sent, jnp.logical_and(oz >= z, z > 0)))
                def _():
                    to_down(oz, ox, p, place(oz, ox, p)).wait_send()

    to_x(z, x, 2, own(2)).wait_send()


def project(
    inputs, query_weight, key_weight, value_weight, adapter_down, adapter_up, out_weight, planes
):
    shard, columns = inputs.shape
    features = 3 * query_weight.shape[0] + adapter_down.shape[0]
    tokens = 2 * shard
    dma = pltpu.SemaphoreType.DMA
    vmem = pl.BlockSpec(memory_space=pltpu.VMEM)
    anywhere = pl.BlockSpec(memory_space=pl.ANY)

    def kernel(*refs):
        project_kernel(planes, *refs)

    return pl.pallas_call(
        kernel,
        out_shape=(
            jax.ShapeDtypeStruct((3 * query_weight.shape[0], tokens), jnp.bfloat16),
            jax.ShapeDtypeStruct((planes,) + out_weight.shape, jnp.bfloat16),
        ),
        in_specs=[anywhere, anywhere, anywhere, anywhere, anywhere, vmem, anywhere],
        out_specs=(vmem, anywhere),
        scratch_shapes=[
            dma((3,)),
            dma((3,)),
            pltpu.VMEM((planes * tokens, columns), jnp.bfloat16),
            pltpu.VMEM((features, columns), jnp.bfloat16),
            pltpu.VMEM((planes, features, tokens), jnp.float32),
            pltpu.VMEM((planes // 2, features, tokens), jnp.float32),
            pltpu.VMEM((features, tokens), jnp.bfloat16),
            pltpu.VMEM((features, tokens), jnp.bfloat16),
            dma((6,)),
            dma((2 * planes, 3)),
            dma((2 * planes, 3)),
            dma((planes, 3)),
            dma((2 * planes, 3)),
            dma((planes // 2, 2)),
            dma((planes // 2, 2)),
            dma((2,)),
            dma((2,)),
        ],
        compiler_params=pltpu.CompilerParams(
            collective_id=0, has_side_effects=True, vmem_limit_bytes=60 * 1024 * 1024
        ),
        cost_estimate=pl.CostEstimate(
            flops=2 * planes * tokens * columns * features,
            bytes_accessed=2 * (planes * tokens + features) * columns,
            transcendentals=0,
        ),
    )(inputs, query_weight, key_weight, value_weight, adapter_down, adapter_up, out_weight)


def output_kernel(
    planes,
    att,
    weight,
    out,
    x_out,
    x_in,
    kept,
    z_out,
    up_in,
    down_in,
    x_send,
    x_recv,
    z_send,
    up_recv,
    down_recv,
):
    z, x = line_position()
    block = out.shape[0]
    greet_line(planes, z, x, ())

    def plane_at(k):
        last = planes - 1
        low = jnp.where(z == 0, last - k, jnp.where(k == 0, 3, jnp.where(k == 1, 0, 3 - k + 1)))
        low = jnp.where(jnp.logical_and(z == 1, k == 3), 1, low)
        m = last - z
        high = jnp.where(m == 0, last - k, jnp.where(k == 0, 3, jnp.where(k == 1, 0, 3 - k + 1)))
        high = jnp.where(jnp.logical_and(m == 1, k == 3), 1, high)
        return jnp.where(z < 2, low, last - high)

    def x_copy(oz):
        return remote(
            x_out.at[oz], x_in.at[oz], x_send.at[oz], x_recv.at[oz], "gy", 2 * z + 1 - x
        )

    def up_copy(oz):
        return remote(
            z_out.at[oz],
            up_in.at[oz],
            z_send.at[oz],
            up_recv.at[oz],
            "gy",
            2 * jnp.minimum(z + 1, planes - 1) + x,
        )

    def down_copy(oz):
        return remote(
            z_out.at[oz],
            down_in.at[oz],
            z_send.at[oz],
            down_recv.at[oz],
            "gy",
            2 * jnp.maximum(z - 1, 0) + x,
        )

    def cross(k, carry):
        oz = plane_at(k)
        both = lax.dot_general(
            weight[oz], att[...], (((0,), (1,)), ((), ())), preferred_element_type=jnp.float32
        )
        low, high = both[:block], both[block:]
        x_out[oz] = jnp.where(x == 0, high, low).astype(x_out.dtype)
        x_copy(oz).start()
        kept[oz] = jnp.where(x == 0, low, high)
        return carry

    lax.fori_loop(0, planes, cross, 0)

    def along(k, carry):
        oz = plane_at(k)
        x_copy(oz).wait_recv()
        kept[oz] = kept[oz] + x_in[oz].astype(jnp.float32)

        @pl.when(jnp.logical_and(z > 0, oz >= z))
        def _():
            up_copy(oz).wait_recv()
            kept[oz] = kept[oz] + up_in[oz].astype(jnp.float32)

        @pl.when(jnp.logical_and(z < planes - 1, oz <= z))
        def _():
            down_copy(oz).wait_recv()
            kept[oz] = kept[oz] + down_in[oz].astype(jnp.float32)

        @pl.when(oz > z)
        def _():
            z_out[oz] = kept[oz].astype(z_out.dtype)
            up_copy(oz).start()

        @pl.when(oz < z)
        def _():
            z_out[oz] = kept[oz].astype(z_out.dtype)
            down_copy(oz).start()

        return carry

    lax.fori_loop(0, planes, along, 0)
    out[...] = kept[z].astype(out.dtype)

    def finish(oz, carry):
        x_copy(oz).wait_send()

        @pl.when(oz != z)
        def _():
            up_copy(oz).wait_send()

        return carry

    lax.fori_loop(0, planes, finish, 0)


def project_out(att, weight, planes):
    tokens = att.shape[0]
    block = weight.shape[2] // 2
    dma = pltpu.SemaphoreType.DMA
    vmem = pl.BlockSpec(memory_space=pltpu.VMEM)
    blocks = (planes, block, tokens)

    def kernel(*refs):
        output_kernel(planes, *refs)

    return pl.pallas_call(
        kernel,
        out_shape=jax.ShapeDtypeStruct((block, tokens), jnp.bfloat16),
        in_specs=[vmem, vmem],
        out_specs=vmem,
        scratch_shapes=[
            pltpu.VMEM(blocks, jnp.bfloat16),
            pltpu.VMEM(blocks, jnp.bfloat16),
            pltpu.VMEM(blocks, jnp.float32),
            pltpu.VMEM(blocks, jnp.bfloat16),
            pltpu.VMEM(blocks, jnp.bfloat16),
            pltpu.VMEM(blocks, jnp.bfloat16),
            dma((planes,)),
            dma((planes,)),
            dma((planes,)),
            dma((planes,)),
            dma((planes,)),
        ],
        compiler_params=pltpu.CompilerParams(
            collective_id=1, has_side_effects=True, vmem_limit_bytes=32 * 1024 * 1024
        ),
    )(att, weight)


def per_device(
    inputs,
    query_weight,
    key_weight,
    value_weight,
    adapter_down,
    adapter_up,
    prompt_keys,
    prompt_values,
    cache_keys,
    cache_values,
    cache_lengths,
    parents,
    out_weight,
):
    requests = cache_keys.shape[0]
    node_count = parents.shape[1]
    local_rows = requests * node_count
    head_width = query_weight.shape[0]
    head_count = head_width // HEAD
    lines = lax.axis_size("gx") == 4 and lax.axis_size("gy") == 8
    shaped = (requests, node_count, head_count, HEAD)
    cached = (requests, head_count, HEAD, cache_keys.shape[2])
    reached = ancestors(parents)
    if lines:
        planes = lax.axis_size("gy") // 2
        projected, columns = project(
            inputs,
            query_weight,
            key_weight,
            value_weight,
            adapter_down,
            adapter_up,
            out_weight,
            planes,
        )
        queries = projected[:head_width].T
        new_keys = projected[head_width : 2 * head_width].T
        new_values = projected[2 * head_width :].T
    else:
        all_rows = lax.all_gather(inputs, "gy", axis=0, tiled=True)
        mixture = lax.psum_scatter(
            jnp.concatenate(
                [
                    contract_rows(all_rows, matrix)
                    for matrix in (query_weight, key_weight, value_weight, adapter_down)
                ],
                axis=1,
            ),
            "gx",
            scatter_dimension=0,
            tiled=True,
        )
        query_base = mixture[:, :head_width]
        new_keys = mixture[:, head_width : 2 * head_width].astype(jnp.bfloat16)
        new_values = mixture[:, 2 * head_width : 3 * head_width].astype(jnp.bfloat16)
        adapter_mid = mixture[:, 3 * head_width :].astype(jnp.bfloat16)
        queries = (query_base + contract_rows(adapter_mid, adapter_up)).astype(jnp.bfloat16)
    attended = attend(
        queries.reshape(shaped),
        new_keys.reshape(shaped),
        new_values.reshape(shaped),
        prompt_keys,
        prompt_values,
        cache_keys.reshape(cached),
        cache_values.reshape(cached),
        cache_lengths,
        reached,
    )
    flattened = attended.reshape(local_rows, head_width)
    if lines:
        return project_out(flattened, columns, planes).T
    partial_sums = jnp.dot(
        flattened,
        lax.all_gather(out_weight, "gx", axis=1, tiled=True),
        preferred_element_type=jnp.float32,
    )
    return lax.psum_scatter(
        partial_sums.astype(jnp.bfloat16), "gy", scatter_dimension=1, tiled=True
    )


def solution(mesh):
    placed = (
        P("gy", "gx"),
        P("gy", "gx"),
        P("gy", "gx"),
        P("gy", "gx"),
        P(None, "gx"),
        P("gy", None),
        P("gx", "gy", None),
        P("gx", "gy", None),
        P("gx", "gy", None),
        P("gx", "gy", None),
        P("gx"),
        P("gx", None),
        P("gy", "gx"),
    )
    return jax.shard_map(
        per_device, mesh=mesh, in_specs=placed, out_specs=P("gx", "gy"), check_vma=False
    )
```

```python
import math

import jax
import jax.numpy as jnp
from jax import lax
from jax.experimental import pallas as pl
from jax.experimental.pallas import tpu as pltpu
from jax.sharding import PartitionSpec as P

HEAD = 224
NT = (((1,), (1,)), ((), ()))
MESH = pl.DeviceIdType.MESH


def contract_rows(left, right):
    return lax.dot_general(left, right, NT, preferred_element_type=jnp.float32)


def ancestors(parents):
    node_count = parents.shape[1]
    columns = jnp.arange(node_count, dtype=jnp.int32)
    parent_hot = (parents[:, :, None] == columns[None, None, :]).astype(jnp.float32)
    reached = jnp.minimum(jnp.eye(node_count, dtype=jnp.float32)[None] + parent_hot, 1.0)
    reached = reached.astype(jnp.bfloat16)
    rounds = max(1, math.ceil(math.log2(node_count)))
    for sweep in range(rounds):
        step = jnp.einsum("rnm,rmk->rnk", reached, reached, preferred_element_type=jnp.float32)
        reached = jnp.minimum(reached.astype(jnp.float32) + step, 1.0).astype(jnp.bfloat16)
    return reached


def attend(queries, new_keys, new_values, prompt_k, prompt_v, cache_k, cache_v, lengths, reached):
    factor = 1.0 / math.sqrt(queries.shape[-1])
    s_prompt = (
        jnp.einsum("rnhe,hep->rnhp", queries, prompt_k, preferred_element_type=jnp.float32) * factor
    )
    s_cache = (
        jnp.einsum("rnhe,rhec->rnhc", queries, cache_k, preferred_element_type=jnp.float32) * factor
    )
    s_tree = (
        jnp.einsum("rnhe,rmhe->rnhm", queries, new_keys, preferred_element_type=jnp.float32)
        * factor
    )
    usable = jnp.arange(cache_k.shape[-1], dtype=jnp.int32)[None, :] < lengths[:, None]
    s_cache = jnp.where(usable[:, None, None, :], s_cache, -jnp.inf)
    s_tree = jnp.where(reached[:, :, None, :] > 0.5, s_tree, -jnp.inf)
    largest = jnp.maximum(
        jnp.maximum(
            jnp.max(s_prompt, axis=-1, keepdims=True), jnp.max(s_cache, axis=-1, keepdims=True)
        ),
        jnp.max(s_tree, axis=-1, keepdims=True),
    )
    e_prompt = jnp.exp(s_prompt - largest)
    e_cache = jnp.exp(s_cache - largest)
    e_tree = jnp.exp(s_tree - largest)
    totals = (
        jnp.sum(e_prompt, axis=-1, keepdims=True)
        + jnp.sum(e_cache, axis=-1, keepdims=True)
        + jnp.sum(e_tree, axis=-1, keepdims=True)
    )
    w_prompt = (e_prompt / totals).astype(jnp.bfloat16)
    w_cache = (e_cache / totals).astype(jnp.bfloat16)
    w_tree = (e_tree / totals).astype(jnp.bfloat16)
    result = jnp.einsum("rnhp,hep->rnhe", w_prompt, prompt_v, preferred_element_type=jnp.float32)
    result = result + jnp.einsum(
        "rnhc,rhec->rnhe", w_cache, cache_v, preferred_element_type=jnp.float32
    )
    result = result + jnp.einsum(
        "rnhm,rmhe->rnhe", w_tree, new_values, preferred_element_type=jnp.float32
    )
    return result.astype(jnp.bfloat16)


def remote(src, dst, send, recv, axis, index):
    return pltpu.make_async_remote_copy(
        src_ref=src,
        dst_ref=dst,
        send_sem=send,
        recv_sem=recv,
        device_id={axis: index},
        device_id_type=MESH,
    )


def line_position():
    h = lax.axis_index("gy")
    z = h // 2
    x = h - 2 * z
    return z, x


def greet_line(planes, z, x, extra):
    barrier = pltpu.get_barrier_semaphore()

    def signal(axis, index):
        pl.semaphore_signal(barrier, inc=1, device_id={axis: index}, device_id_type=MESH)

    signal("gy", 2 * z + 1 - x)
    for index in extra:
        signal("gx", index)

    @pl.when(z > 0)
    def _():
        signal("gy", 2 * (z - 1) + x)

    @pl.when(z < planes - 1)
    def _():
        signal("gy", 2 * (z + 1) + x)

    inner = jnp.where(z > 0, 1, 0) + jnp.where(z < planes - 1, 1, 0)
    pl.semaphore_wait(barrier, 1 + len(extra) + inner)


def pieces_of(rows):
    late = rows // 6
    half = (rows - late) // 2
    return ((0, half), (half, half), (2 * half, late))


def project_kernel(
    planes,
    x_ref,
    wq,
    wk,
    wv,
    wd,
    up,
    wo,
    out,
    cols,
    spread_send,
    spread_recv,
    rows_buf,
    weights,
    part,
    core_in,
    y_out,
    y_in,
    w_sem,
    up_send,
    down_send,
    x_send,
    recv,
    c_send,
    c_recv,
    y_send,
    y_recv,
):
    z, x = line_position()
    mine = lax.axis_index("gx")
    y = mine // 2
    core = mine - 2 * y
    other_core = 2 * y + 1 - core
    other_y = 2 * (1 - y) + core
    shard = x_ref.shape[0]
    group_rows = 2 * shard
    ranges = pieces_of(shard)
    width = wq.shape[0]

    loads = []
    start = 0
    for slot, matrix in enumerate((wq, wk, wv, wd)):
        count = matrix.shape[0]
        load = pltpu.make_async_copy(
            matrix, weights.at[pl.ds(start, count)], w_sem.at[slot]
        )
        load.start()
        loads.append(load)
        start += count

    greet_line(planes, z, x, (other_core, other_y))

    own_block = pltpu.make_async_copy(wo, cols.at[mine], w_sem.at[5])

    def block_copy(slot, index, target, src):
        return remote(
            src, cols.at[index], spread_send.at[slot], spread_recv.at[slot], "gx", target
        )

    def spread_start():
        own_block.start()
        block_copy(0, mine, other_y, wo).start()
        block_copy(1, mine, other_core, wo).start()

    def spread_second():
        block_copy(0, other_y, other_y, cols.at[other_y]).wait_recv()
        block_copy(2, other_y, other_core, cols.at[other_y]).start()

    def spread_end():
        own_block.wait()
        block_copy(0, mine, other_y, wo).wait_send()
        block_copy(1, mine, other_core, wo).wait_send()
        block_copy(2, other_y, other_core, cols.at[other_y]).wait_send()
        block_copy(1, other_core, other_core, cols.at[other_core]).wait_recv()
        cross = 2 * (1 - y) + 1 - core
        block_copy(2, cross, other_core, cols.at[cross]).wait_recv()

    def place(oz, ox, p):
        first, count = ranges[p]
        return rows_buf.at[pl.ds(pl.multiple_of((2 * oz + ox) * shard + first, 16), count)]

    def own(p):
        first, count = ranges[p]
        return x_ref.at[pl.ds(first, count)]

    def to_x(oz, ox, p, src):
        return remote(
            src, place(oz, ox, p), x_send.at[oz, p], recv.at[2 * oz + ox, p], "gy", 2 * z + 1 - x
        )

    def to_up(oz, ox, p, src):
        return remote(
            src,
            place(oz, ox, p),
            up_send.at[2 * oz + ox, p],
            recv.at[2 * oz + ox, p],
            "gy",
            2 * jnp.minimum(z + 1, planes - 1) + x,
        )

    def to_down(oz, ox, p, src):
        return remote(
            src,
            place(oz, ox, p),
            down_send.at[2 * oz + ox, p],
            recv.at[2 * oz + ox, p],
            "gy",
            2 * jnp.maximum(z - 1, 0) + x,
        )

    def arrived(oz, ox, p):
        ref = place(oz, ox, p)
        remote(ref, ref, x_send.at[0, 0], recv.at[2 * oz + ox, p], "gy", 2 * z + 1 - x).wait_recv()

    def both_ways(oz, ox, p, src):
        @pl.when(z < planes - 1)
        def _():
            to_up(oz, ox, p, src).start()

        @pl.when(z > 0)
        def _():
            to_down(oz, ox, p, src).start()

    to_x(z, x, 2, own(2)).start()
    for p in (0, 1, 2):
        both_ways(z, x, p, own(p))
        if p < 2:
            to_x(z, x, p, own(p)).start()
    mine_copy = pltpu.make_async_copy(
        x_ref, rows_buf.at[pl.ds(pl.multiple_of((2 * z + x) * shard, 16), shard)], w_sem.at[4]
    )
    mine_copy.start()
    spread_start()
    arrived(z, 1 - x, 2)
    both_ways(z, 1 - x, 2, place(z, 1 - x, 2))
    for load in loads:
        load.wait()
    mine_copy.wait()

    def from_side(oz, below, p, ox):
        @pl.when(jnp.logical_and(oz >= 0, oz < planes))
        def _():
            arrived(oz, ox, p)
            src = place(oz, ox, p)
            if below:

                @pl.when(z < planes - 1)
                def _():
                    to_up(oz, ox, p, src).start()
            else:

                @pl.when(z > 0)
                def _():
                    to_down(oz, ox, p, src).start()

    def from_sides(distance, p, ox, cross):
        for below in (True, False):
            oz = z - distance if below else z + distance
            from_side(oz, below, p, ox)
            if cross:

                @pl.when(jnp.logical_and(oz >= 0, oz < planes))
                def _():
                    to_x(oz, x, p, place(oz, x, p)).start()

    def group_at(k):
        last = planes - 1
        low = jnp.where(z == 0, k, jnp.where(k == 0, 1, jnp.where(k == 1, 0, k)))
        m = last - z
        high = jnp.where(m == 0, k, jnp.where(k == 0, 1, jnp.where(k == 1, 0, k)))
        return jnp.where(z < 2, low, last - high)

    span = weights.shape[0] // 2

    def core_copy(g, i):
        lines = pl.ds(i * span, span)
        return remote(
            part.at[g, lines],
            core_in.at[g // 2, lines],
            c_send.at[g // 2, i],
            c_recv.at[g // 2, i],
            "gx",
            other_core,
        )

    def y_copy(i):
        lines = pl.ds(i * span, span)
        return remote(y_out.at[lines], y_in.at[lines], y_send.at[i], y_recv.at[i], "gx", other_y)

    def settle(g):
        @pl.when(g - 2 * (g // 2) == core)
        def _():
            for i in (0, 1):
                lines = pl.ds(i * span, span)
                core_copy(g, i).wait_recv()

                @pl.when(g // 2 != y)
                def _():
                    y_out[lines] = (part[g, lines] + core_in[g // 2, lines]).astype(y_out.dtype)
                    y_copy(i).start()

    def step(k, carry):
        distance = k + 1
        for p in (0, 1):
            from_sides(distance, p, x, True)
        for ox in (x, 1 - x):
            from_sides(distance, 2, ox, False)

        @pl.when(k > 0)
        def _():
            settle(group_at(k - 1))

        @pl.when(k == 1)
        def _():
            spread_second()

        g = group_at(k)
        for p in (0, 1):
            arrived(g, 1 - x, p)
        for i in (0, 1):
            lines = pl.ds(i * span, span)
            part[g, lines] = lax.dot_general(
                weights[lines],
                rows_buf[pl.ds(pl.multiple_of(g * group_rows, 16), group_rows)],
                NT,
                preferred_element_type=jnp.float32,
            )

            @pl.when(g - 2 * (g // 2) != core)
            def _():
                core_copy(g, i).start()

        return carry

    lax.fori_loop(0, planes, step, 0)
    settle(group_at(planes - 1))
    y_copy(0).wait_recv()
    y_copy(1).wait_recv()
    total = part[mine] + core_in[mine // 2] + y_in[...].astype(jnp.float32)
    middle = total[3 * width :].astype(jnp.bfloat16)
    extra = jnp.dot(up[...], middle, preferred_element_type=jnp.float32)
    out[0] = (total[:width] + extra).T.astype(jnp.bfloat16)
    out[1] = total[width : 2 * width].T.astype(jnp.bfloat16)
    out[2] = total[2 * width : 3 * width].T.astype(jnp.bfloat16)

    spread_end()
    y_copy(0).wait_send()
    y_copy(1).wait_send()
    for half in range(planes // 2):
        core_copy(2 * half + 1 - core, 0).wait_send()
        core_copy(2 * half + 1 - core, 1).wait_send()
    for oz in range(planes):
        for p in (0, 1):
            to_x(oz, x, p, place(oz, x, p)).wait_send()
        for ox in (0, 1):
            for p in (0, 1, 2):
                if p == 2:
                    sent = oz >= 0
                else:
                    sent = x == ox

                @pl.when(jnp.logical_and(sent, jnp.logical_and(oz <= z, z < planes - 1)))
                def _():
                    to_up(oz, ox, p, place(oz, ox, p)).wait_send()

                @pl.when(jnp.logical_and(sent, jnp.logical_and(oz >= z, z > 0)))
                def _():
                    to_down(oz, ox, p, place(oz, ox, p)).wait_send()

    to_x(z, x, 2, own(2)).wait_send()


def project(
    inputs, query_weight, key_weight, value_weight, adapter_down, adapter_up, out_weight, planes
):
    shard, columns = inputs.shape
    features = 3 * query_weight.shape[0] + adapter_down.shape[0]
    tokens = 2 * shard
    dma = pltpu.SemaphoreType.DMA
    vmem = pl.BlockSpec(memory_space=pltpu.VMEM)
    anywhere = pl.BlockSpec(memory_space=pl.ANY)

    def kernel(*refs):
        project_kernel(planes, *refs)

    return pl.pallas_call(
        kernel,
        out_shape=(
            jax.ShapeDtypeStruct((3, tokens, query_weight.shape[0]), jnp.bfloat16),
            jax.ShapeDtypeStruct((planes,) + out_weight.shape, jnp.bfloat16),
        ),
        in_specs=[anywhere, anywhere, anywhere, anywhere, anywhere, vmem, anywhere],
        out_specs=(vmem, anywhere),
        scratch_shapes=[
            dma((3,)),
            dma((3,)),
            pltpu.VMEM((planes * tokens, columns), jnp.bfloat16),
            pltpu.VMEM((features, columns), jnp.bfloat16),
            pltpu.VMEM((planes, features, tokens), jnp.float32),
            pltpu.VMEM((planes // 2, features, tokens), jnp.float32),
            pltpu.VMEM((features, tokens), jnp.bfloat16),
            pltpu.VMEM((features, tokens), jnp.bfloat16),
            dma((6,)),
            dma((2 * planes, 3)),
            dma((2 * planes, 3)),
            dma((planes, 3)),
            dma((2 * planes, 3)),
            dma((planes // 2, 2)),
            dma((planes // 2, 2)),
            dma((2,)),
            dma((2,)),
        ],
        compiler_params=pltpu.CompilerParams(
            collective_id=0, has_side_effects=True, vmem_limit_bytes=60 * 1024 * 1024
        ),
        cost_estimate=pl.CostEstimate(
            flops=2 * planes * tokens * columns * features,
            bytes_accessed=2 * (planes * tokens + features) * columns,
            transcendentals=0,
        ),
    )(inputs, query_weight, key_weight, value_weight, adapter_down, adapter_up, out_weight)


def output_kernel(
    planes,
    att,
    weight,
    out,
    x_out,
    x_in,
    kept,
    z_out,
    up_in,
    down_in,
    x_send,
    x_recv,
    z_send,
    up_recv,
    down_recv,
):
    z, x = line_position()
    block = out.shape[0]
    greet_line(planes, z, x, ())

    def plane_at(k):
        last = planes - 1
        low = jnp.where(z == 0, last - k, jnp.where(k == 0, 3, jnp.where(k == 1, 0, 3 - k + 1)))
        low = jnp.where(jnp.logical_and(z == 1, k == 3), 1, low)
        m = last - z
        high = jnp.where(m == 0, last - k, jnp.where(k == 0, 3, jnp.where(k == 1, 0, 3 - k + 1)))
        high = jnp.where(jnp.logical_and(m == 1, k == 3), 1, high)
        return jnp.where(z < 2, low, last - high)

    def x_copy(oz):
        return remote(
            x_out.at[oz], x_in.at[oz], x_send.at[oz], x_recv.at[oz], "gy", 2 * z + 1 - x
        )

    def up_copy(oz):
        return remote(
            z_out.at[oz],
            up_in.at[oz],
            z_send.at[oz],
            up_recv.at[oz],
            "gy",
            2 * jnp.minimum(z + 1, planes - 1) + x,
        )

    def down_copy(oz):
        return remote(
            z_out.at[oz],
            down_in.at[oz],
            z_send.at[oz],
            down_recv.at[oz],
            "gy",
            2 * jnp.maximum(z - 1, 0) + x,
        )

    def cross(k, carry):
        oz = plane_at(k)
        both = lax.dot_general(
            weight[oz], att[...], (((0,), (1,)), ((), ())), preferred_element_type=jnp.float32
        )
        low, high = both[:block], both[block:]
        x_out[oz] = jnp.where(x == 0, high, low).astype(x_out.dtype)
        x_copy(oz).start()
        kept[oz] = jnp.where(x == 0, low, high)
        return carry

    lax.fori_loop(0, planes, cross, 0)

    def along(k, carry):
        oz = plane_at(k)
        x_copy(oz).wait_recv()
        kept[oz] = kept[oz] + x_in[oz].astype(jnp.float32)

        @pl.when(jnp.logical_and(z > 0, oz >= z))
        def _():
            up_copy(oz).wait_recv()
            kept[oz] = kept[oz] + up_in[oz].astype(jnp.float32)

        @pl.when(jnp.logical_and(z < planes - 1, oz <= z))
        def _():
            down_copy(oz).wait_recv()
            kept[oz] = kept[oz] + down_in[oz].astype(jnp.float32)

        @pl.when(oz > z)
        def _():
            z_out[oz] = kept[oz].astype(z_out.dtype)
            up_copy(oz).start()

        @pl.when(oz < z)
        def _():
            z_out[oz] = kept[oz].astype(z_out.dtype)
            down_copy(oz).start()

        return carry

    lax.fori_loop(0, planes, along, 0)
    out[...] = kept[z].astype(out.dtype)

    def finish(oz, carry):
        x_copy(oz).wait_send()

        @pl.when(oz != z)
        def _():
            up_copy(oz).wait_send()

        return carry

    lax.fori_loop(0, planes, finish, 0)


def project_out(att, weight, planes):
    tokens = att.shape[0]
    block = weight.shape[2] // 2
    dma = pltpu.SemaphoreType.DMA
    vmem = pl.BlockSpec(memory_space=pltpu.VMEM)
    blocks = (planes, block, tokens)

    def kernel(*refs):
        output_kernel(planes, *refs)

    return pl.pallas_call(
        kernel,
        out_shape=jax.ShapeDtypeStruct((block, tokens), jnp.bfloat16),
        in_specs=[vmem, vmem],
        out_specs=vmem,
        scratch_shapes=[
            pltpu.VMEM(blocks, jnp.bfloat16),
            pltpu.VMEM(blocks, jnp.bfloat16),
            pltpu.VMEM(blocks, jnp.float32),
            pltpu.VMEM(blocks, jnp.bfloat16),
            pltpu.VMEM(blocks, jnp.bfloat16),
            pltpu.VMEM(blocks, jnp.bfloat16),
            dma((planes,)),
            dma((planes,)),
            dma((planes,)),
            dma((planes,)),
            dma((planes,)),
        ],
        compiler_params=pltpu.CompilerParams(
            collective_id=1, has_side_effects=True, vmem_limit_bytes=32 * 1024 * 1024
        ),
    )(att, weight)


def per_device(
    inputs,
    query_weight,
    key_weight,
    value_weight,
    adapter_down,
    adapter_up,
    prompt_keys,
    prompt_values,
    cache_keys,
    cache_values,
    cache_lengths,
    parents,
    out_weight,
):
    requests = cache_keys.shape[0]
    node_count = parents.shape[1]
    local_rows = requests * node_count
    head_width = query_weight.shape[0]
    head_count = head_width // HEAD
    lines = lax.axis_size("gx") == 4 and lax.axis_size("gy") == 8
    shaped = (requests, node_count, head_count, HEAD)
    cached = (requests, head_count, HEAD, cache_keys.shape[2])
    reached = ancestors(parents)
    if lines:
        planes = lax.axis_size("gy") // 2
        projected, columns = project(
            inputs,
            query_weight,
            key_weight,
            value_weight,
            adapter_down,
            adapter_up,
            out_weight,
            planes,
        )
        queries = projected[0]
        new_keys = projected[1]
        new_values = projected[2]
    else:
        all_rows = lax.all_gather(inputs, "gy", axis=0, tiled=True)
        mixture = lax.psum_scatter(
            jnp.concatenate(
                [
                    contract_rows(all_rows, matrix)
                    for matrix in (query_weight, key_weight, value_weight, adapter_down)
                ],
                axis=1,
            ),
            "gx",
            scatter_dimension=0,
            tiled=True,
        )
        query_base = mixture[:, :head_width]
        new_keys = mixture[:, head_width : 2 * head_width].astype(jnp.bfloat16)
        new_values = mixture[:, 2 * head_width : 3 * head_width].astype(jnp.bfloat16)
        adapter_mid = mixture[:, 3 * head_width :].astype(jnp.bfloat16)
        queries = (query_base + contract_rows(adapter_mid, adapter_up)).astype(jnp.bfloat16)
    attended = attend(
        queries.reshape(shaped),
        new_keys.reshape(shaped),
        new_values.reshape(shaped),
        prompt_keys,
        prompt_values,
        cache_keys.reshape(cached),
        cache_values.reshape(cached),
        cache_lengths,
        reached,
    )
    flattened = attended.reshape(local_rows, head_width)
    if lines:
        return project_out(flattened, columns, planes).T
    partial_sums = jnp.dot(
        flattened,
        lax.all_gather(out_weight, "gx", axis=1, tiled=True),
        preferred_element_type=jnp.float32,
    )
    return lax.psum_scatter(
        partial_sums.astype(jnp.bfloat16), "gy", scatter_dimension=1, tiled=True
    )


def solution(mesh):
    placed = (
        P("gy", "gx"),
        P("gy", "gx"),
        P("gy", "gx"),
        P("gy", "gx"),
        P(None, "gx"),
        P("gy", None),
        P("gx", "gy", None),
        P("gx", "gy", None),
        P("gx", "gy", None),
        P("gx", "gy", None),
        P("gx"),
        P("gx", None),
        P("gy", "gx"),
    )
    return jax.shard_map(
        per_device, mesh=mesh, in_specs=placed, out_specs=P("gx", "gy"), check_vma=False
    )
```
